32 devices in a mesh: groups: 2 (over x), expert: 8 (over z, y), dp: 2 (over core).
Axes of the slice: x: 2, y: 2, z: 4, core: 2. Of those that a mesh axis runs over, the one named last changes fastest.
Arguments:
- tokens: bfloat16 [4096, 1536], P(('groups', 'expert', 'dp')), parts along dimension 0, may hold values from -6 to 6
- cotangent: bfloat16 [4096, 1536], P(('groups', 'expert', 'dp')), parts along dimension 0, may hold values from -6 to 6
- mixture: bfloat16 [4096, 1536], P(('groups', 'expert', 'dp')), parts along dimension 0, may hold values from -3 to 3
- stamp: int32 [4096], P(('groups', 'expert', 'dp')), parts along dimension 0, may hold values from 0 to 31
- expert_ids: int32 [4096, 2], P(('groups', 'expert', 'dp')), parts along dimension 0, may hold values from 0 to 7, all different within a row; in each aligned block of 128 rows (0 to 127, 128 to 255, ...) at most 64 rows name the same one
- modulation: float32 [3, 32, 1536], replicated, may hold values from -3 to 3
- router: bfloat16 [8, 1536], replicated, may hold values from -0.15625 to 0.15625
- w_gate: bfloat16 [8, 1536, 768], P('expert', None, 'dp'), may hold values from -0.15625 to 0.15625
- w_up: bfloat16 [8, 1536, 768], P('expert', None, 'dp'), may hold values from -0.15625 to 0.15625
- w_down: bfloat16 [8, 1536, 768], P('expert', None, 'dp'), may hold values from -0.21875 to 0.21875
Outputs:
- d_tokens: bfloat16 [4096, 1536], P(('groups', 'expert', 'dp')), parts along dimension 0
- d_gate_w: bfloat16 [16, 1536, 768], P(('groups', 'expert'), None, 'dp'), parts along dimension 0
- d_up_w: bfloat16 [16, 1536, 768], P(('groups', 'expert'), None, 'dp'), parts along dimension 0
- d_down_w: bfloat16 [16, 1536, 768], P(('groups', 'expert'), None, 'dp'), parts along dimension 0
- d_router: float32 [16, 1536], P('groups'), parts along dimension 0
- d_modulation: float32 [3, 64, 1536], P(None, 'groups'), parts along dimension 1
The draws below stay inside these ranges and needn't reach their ends.
There are 2 independent parts, one for each index of `groups`. The reference program is written for one: setup_inputs(seed, part) draws one part's arguments, and reference() takes and returns one part's arrays. A program takes and returns all parts, laid end to end along the dimension named above; an argument that names none is the same for every part. Nothing has to cross between parts.
Inputs may be any that keep to these rules, and one draw needn't show every extreme that they name: `expert_ids`: each token names two different experts. Within the tokens of one device (aligned blocks of 128 tokens) no expert is named more than 64 times, and in every draw some expert is named exactly 64 times in some block.
All inputs are finite; a program needn't handle non-finite values.
Results may differ from the reference program's by a relative error of at most 0.015.
Values may be sent and summed in bfloat16 or wider, within the bound.
No kernel may reach another device: no remote copies, remote signals or barrier semaphores. Data moves between devices by JAX's collectives and lax.ppermute only.
A program may use at most 128 MiB of HBM per device.

```python
import math
import jax
import jax.numpy as jnp
import numpy as np
from jax import lax

D = 1536
FF = 768
TOK_DEV = 128
COND = 32
EXPERTS = 8
CAP = 64
TOKENS = 2048


def place_ends(drawn, key, least, top_value):
    longest = drawn.shape.index(max(drawn.shape))
    spots = []
    for shift in (0, 1):
        where = [jax.random.randint(jax.random.fold_in(key, axis), (), 0, length) for axis, length in enumerate(drawn.shape)]
        where[longest] = (where[longest] + shift) % drawn.shape[longest]
        spots.append(tuple(where))
    return drawn.at[spots[0]].set(least).at[spots[1]].set(top_value)


def levels(key, shape, split, low, top_value):
    factor_of, own = 1.0, jax.random.fold_in(key, 6)
    for dim, parts in split:
        steps = jnp.exp(jax.random.uniform(jax.random.fold_in(own, dim), (parts,), jnp.float32, low / len(split), top_value / len(split)))
        factor_of = factor_of * jnp.repeat(steps, shape[dim] // parts).reshape([-1 if axis == dim else 1 for axis in range(len(shape))])
    return factor_of


def shared_out(rng, own, number, rows, count, top, limit, lean):
    sequence = jax.random.permutation(rng, count)
    heavy_load, common = load_shares(count, rows * top, limit, lean, True), load_shares(count, rows * top, limit, lean, False)
    places = jnp.arange(count)

    def named(lengths, turn):
        used = int((lengths > 0).sum())
        fixed = max(1, used // 4)
        shifted = fixed + (places - fixed + turn * (used - fixed)) % max(1, count - fixed)
        return jnp.zeros((count,), jnp.int32).at[sequence[jnp.where(places < fixed, places, shifted)]].set(jnp.asarray(lengths, jnp.int32))

    lengths = jnp.where(number % 4 == 0, named(heavy_load, number // 4), named(common, number - number // 4 - 1))
    mixed = jax.random.permutation(jax.random.fold_in(own, 3), count)
    source_of, receiver = mixed[0:count // 2 * 2:2], mixed[1:count // 2 * 2:2]
    margin = jnp.minimum(lengths[source_of] - 1, limit - lengths[receiver]) // 2
    margin = jnp.where((source_of == sequence[0]) | (receiver == sequence[0]) | (lengths[receiver] == 0), 0, jnp.maximum(margin, 0))
    shifted = jax.random.randint(jax.random.fold_in(own, 4), (count // 2,), 0, 1 << 20) % (margin + 1)
    lengths = lengths.at[source_of].add(-shifted).at[receiver].add(shifted)
    items = jnp.searchsorted(jnp.cumsum(lengths), jnp.arange(rows * top), side="right").astype(jnp.int32)
    listing = items.reshape(top, rows).T
    listing = listing[jax.random.permutation(jax.random.fold_in(own, 1), rows)]
    turn = jax.random.randint(jax.random.fold_in(own, 2), (rows, 1), 0, top)
    return jnp.take_along_axis(listing, (jnp.arange(top)[None, :] + turn) % top, axis=1)


def load_shares(count, total, reach, lean, full):
    portions = [(1 << 20) // math.isqrt(standing ** lean) + 1 for standing in range(1, count + 1)]
    largest = reach if full else min(reach, max(-(-total // count), total * portions[0] // sum(portions)))
    least = 1 if total - largest >= count - 1 else 0
    given, rest = [largest] + [least] * (count - 1), total - largest - least * (count - 1)
    while rest > 0:
        free = [i for i in range(1, count) if given[i] < largest] or [i for i in range(1, count) if given[i] < reach]
        whole, remaining = sum([portions[i] for i in free]), rest
        for i in free:
            extra = min(reach - given[i], max(1, remaining * portions[i] // whole), rest)
            given[i] = given[i] + extra
            rest = rest - extra
    return np.array(given)


def gaussian(own_key, dims, scale, limit, split=(), kind=jnp.bfloat16):
    level = levels(own_key, dims, split, -0.22, 0.18) if split else 1.0
    array = jax.random.normal(own_key, dims, jnp.float32) * scale * level
    return jnp.minimum(jnp.maximum(array, -limit), limit).astype(kind)


def setup_inputs(seed: int = 0, part: int = 0) -> dict:
    key_list = jax.random.split(jax.random.key(seed), 11)
    own_keys = jax.random.split(jax.random.fold_in(key_list[10], part), 11)
    tokens = gaussian(own_keys[0], (TOKENS, D), 1.0, 6.0, ((0, 16),))
    cotangent = gaussian(own_keys[1], (TOKENS, D), 1.0, 6.0, ((0, 16),))
    mixture = gaussian(own_keys[2], (TOKENS, D), 0.5, 3.0, ((0, 16),))
    stamp = place_ends(jax.random.randint(own_keys[3], (TOKENS,), 0, COND), jax.random.fold_in(own_keys[3], 1), 0, COND - 1).astype(jnp.int32)
    expert_ids_keys = jax.random.split(jax.random.fold_in(own_keys[4], 1), TOKENS // TOK_DEV)
    expert_ids_turns = jax.random.permutation(jax.random.fold_in(own_keys[4], 3), TOKENS // TOK_DEV)
    expert_ids = jax.vmap(lambda own, number: shared_out(jax.random.fold_in(own_keys[4], 2), own, number, TOK_DEV, EXPERTS, 2, CAP, 2))(expert_ids_keys, expert_ids_turns).reshape((TOKENS, 2))
    modulation = gaussian(key_list[5], (3, COND, D), 0.5, 3.0, (), jnp.float32)
    router = gaussian(key_list[6], (EXPERTS, D), D ** -0.5, 0.15625)
    w_gate = gaussian(key_list[7], (EXPERTS, D, FF), D ** -0.5, 0.15625, ((0, 8), (2, 2)))
    w_up = gaussian(key_list[8], (EXPERTS, D, FF), D ** -0.5, 0.15625, ((0, 8), (2, 2)))
    w_down = gaussian(key_list[9], (EXPERTS, D, FF), FF ** -0.5, 0.21875, ((0, 8), (2, 2)))
    return {"tokens": tokens, "cotangent": cotangent, "mixture": mixture, "stamp": stamp, "expert_ids": expert_ids, "modulation": modulation, "router": router, "w_gate": w_gate, "w_up": w_up, "w_down": w_down}


epsilon = 1e-06
highest = lax.Precision.HIGHEST

def normalize(tokens):
    values = tokens.astype(jnp.float32)
    centred = values - lax.optimization_barrier(jnp.mean(values, axis=-1, keepdims=True))
    inverse = lax.rsqrt(lax.optimization_barrier(jnp.mean(centred * centred, axis=-1, keepdims=True)) + epsilon)
    return (centred * inverse, inverse)

def slot_positions(flat_ids, tok_count, experts):
    blocked = flat_ids.reshape(-1, 2 * tok_count)
    onehot = (blocked[:, :, None] == jnp.arange(experts, dtype=jnp.int32)).astype(jnp.int32)
    before = jnp.cumsum(onehot, axis=1) - onehot
    return lax.optimization_barrier(jnp.sum(before * onehot, axis=2)).reshape(-1).astype(jnp.int32)

def expert_backward(in_rows, cot_rows, prob_rows, gate_weight, up_weight, down_weight):
    contract_one = (((1,), (1,)), ((), ()))
    contract_zero = (((0,), (0,)), ((), ()))
    pre_gate = jnp.dot(in_rows, gate_weight, preferred_element_type=jnp.float32)
    pre_up = jnp.dot(in_rows, up_weight, preferred_element_type=jnp.float32)
    sigmoid_gate = jax.nn.sigmoid(pre_gate)
    active = pre_gate * sigmoid_gate
    hidden = (active * pre_up).astype(jnp.bfloat16)
    out_grad = (prob_rows[:, None] * cot_rows.astype(jnp.float32)).astype(jnp.bfloat16)
    output = lax.dot_general(hidden, down_weight, contract_one, preferred_element_type=jnp.float32)
    prob_grad = lax.optimization_barrier(jnp.sum(cot_rows.astype(jnp.float32) * output, axis=1))
    hidden_grad = jnp.dot(out_grad, down_weight, preferred_element_type=jnp.float32)
    gate_grad = (hidden_grad * pre_up * sigmoid_gate * (1.0 + pre_gate * (1.0 - sigmoid_gate))).astype(jnp.bfloat16)
    up_grad = (hidden_grad * active).astype(jnp.bfloat16)
    grad_gate = lax.dot_general(in_rows, gate_grad, contract_zero, preferred_element_type=jnp.float32)
    grad_up = lax.dot_general(in_rows, up_grad, contract_zero, preferred_element_type=jnp.float32)
    grad_down = lax.dot_general(out_grad, hidden, contract_zero, preferred_element_type=jnp.float32)
    row_grad = lax.dot_general(gate_grad, gate_weight, contract_one, preferred_element_type=jnp.float32)
    row_grad = row_grad + lax.dot_general(up_grad, up_weight, contract_one, preferred_element_type=jnp.float32)
    return (row_grad, prob_grad, grad_gate, grad_up, grad_down)

def reference(tokens, cotangent, mixture, stamp, expert_ids, modulation, router, w_gate, w_up, w_down):
    tok_total = tokens.shape[0]
    normed, inverse = normalize(tokens)
    shift_rows = modulation[0][stamp]
    scale_rows = modulation[1][stamp]
    gate_rows = modulation[2][stamp]
    modulated = (normed * (1.0 + scale_rows) + shift_rows).astype(jnp.bfloat16)
    upstream = (gate_rows * cotangent.astype(jnp.float32)).astype(jnp.bfloat16)
    logits = lax.dot_general(modulated, router, (((1,), (1,)), ((), ())), preferred_element_type=jnp.float32)
    chosen_prob = jax.nn.sigmoid(jnp.take_along_axis(logits, expert_ids, axis=1))
    flat_ids = expert_ids.reshape(-1).astype(jnp.int32)
    slot_index = slot_positions(flat_ids, TOK_DEV, EXPERTS)
    row_index = jnp.arange(2 * tok_total, dtype=jnp.int32)
    block_count = tok_total // TOK_DEV
    places = row_index // (2 * TOK_DEV) * CAP + slot_index
    pick_table = jnp.full((EXPERTS, block_count * CAP), 2 * tok_total, jnp.int32)
    pick_table = pick_table.at[flat_ids, places].set(row_index)
    in_padded = jnp.concatenate([jnp.repeat(modulated, 2, axis=0), jnp.zeros((1, D), jnp.bfloat16)], axis=0)
    cot_padded = jnp.concatenate([jnp.repeat(upstream, 2, axis=0), jnp.zeros((1, D), jnp.bfloat16)], axis=0)
    prob_padded = jnp.concatenate([chosen_prob.reshape(-1), jnp.zeros((1,), jnp.float32)], axis=0)

    def per_expert(operands):
        row_picks, gate_weight, up_weight, down_weight = operands
        return expert_backward(in_padded[row_picks], cot_padded[row_picks], prob_padded[row_picks], gate_weight, up_weight, down_weight)
    row_grad, prob_grad, grad_gate, grad_up, grad_down = lax.map(per_expert, (pick_table, w_gate, w_up, w_down))
    back_rows = row_grad.astype(jnp.bfloat16)[flat_ids, places].astype(jnp.float32).reshape(tok_total, 2, D)
    back_prob = prob_grad[flat_ids, places].reshape(tok_total, 2)
    logit_grad = back_prob * chosen_prob * (1.0 - chosen_prob)
    onehot_e = (expert_ids[:, :, None] == jnp.arange(EXPERTS, dtype=jnp.int32)).astype(jnp.float32)
    logit_table = lax.optimization_barrier(jnp.sum(onehot_e * logit_grad[:, :, None], axis=1))
    mod_grad = lax.optimization_barrier(jnp.sum(back_rows, axis=1)) + jnp.dot(logit_table, router.astype(jnp.float32), precision=highest)
    d_router = jnp.dot(logit_table.T, modulated.astype(jnp.float32), precision=highest)
    d_normed = mod_grad * (1.0 + scale_rows)
    d_input = inverse * (d_normed - lax.optimization_barrier(jnp.mean(d_normed, axis=-1, keepdims=True)) - normed * lax.optimization_barrier(jnp.mean(d_normed * normed, axis=-1, keepdims=True)))
    d_tokens = (cotangent.astype(jnp.float32) + d_input).astype(jnp.bfloat16)
    onehot_t = (stamp[:, None] == jnp.arange(COND, dtype=jnp.int32)).astype(jnp.float32)
    gate_terms = cotangent.astype(jnp.float32) * mixture.astype(jnp.float32)
    d_modulation = jnp.stack([jnp.dot(onehot_t.T, mod_grad, precision=highest), jnp.dot(onehot_t.T, mod_grad * normed, precision=highest), jnp.dot(onehot_t.T, gate_terms, precision=highest)])
    return (d_tokens, grad_gate.astype(jnp.bfloat16), grad_up.astype(jnp.bfloat16), grad_down.astype(jnp.bfloat16), d_router, d_modulation)
```

```python
import functools

import jax
import jax.numpy as jnp
from jax import lax
from jax.experimental import pallas as pl
from jax.experimental.pallas import tpu as pltpu
from jax.sharding import PartitionSpec as P

epsilon = 1e-06
f32 = jnp.float32
bf16 = jnp.bfloat16
LANES = 128
VMEM = pl.BlockSpec(memory_space=pltpu.VMEM)
SMEM = pl.BlockSpec(memory_space=pltpu.SMEM)
ANY = pl.BlockSpec(memory_space=pl.ANY)


def params(mib):
    return pltpu.CompilerParams(vmem_limit_bytes=mib * 1024 * 1024)


def cost(flops, moved):
    return pl.CostEstimate(flops=int(flops), bytes_accessed=int(moved), transcendentals=0)


def dot(a, b, dims=((1,), (0,))):
    return lax.dot_general(a, b, (dims, ((), ())), preferred_element_type=f32)


def routing(me, meta_ref, count, cap):
    toks = meta_ref.shape[1]
    height = max(8, count)
    wanted = jnp.bitwise_xor(me, lax.broadcasted_iota(jnp.int32, (height, toks), 0))
    member = jnp.logical_or(meta_ref[0:1, :] == wanted, meta_ref[1:2, :] == wanted)
    earlier = lax.broadcasted_iota(jnp.int32, (toks, toks), 0) < lax.broadcasted_iota(
        jnp.int32, (toks, toks), 1
    )
    slots = dot(member.astype(f32).astype(bf16), earlier.astype(f32).astype(bf16))
    slots = jnp.where(member, slots, -1.0).astype(jnp.int32)
    place = lax.broadcasted_iota(jnp.int32, (cap, toks), 0)
    return [(slots[k : k + 1, :] == place).astype(f32) for k in range(count)]


def split3(table):
    high = table.astype(bf16)
    rest = table - high.astype(f32)
    middle = rest.astype(bf16)
    low = (rest - middle.astype(f32)).astype(bf16)
    return jnp.concatenate([high, middle, low], axis=0)


def pick3(column, conditions):
    lane = lax.broadcasted_iota(jnp.int32, (column.shape[0], 3 * conditions), 1)
    return (lax.rem(lane, conditions) + 1 == column.astype(jnp.int32)).astype(f32).astype(bf16)


def own_row(me, router_ref):
    table = router_ref[...].astype(f32)
    place = lax.broadcasted_iota(jnp.int32, table.shape, 0)
    return jnp.sum(jnp.where(place == me, table, 0.0), axis=0, keepdims=True)


def normalize(values):
    mean = jnp.mean(values, axis=-1, keepdims=True)
    centred = values - mean
    inverse = lax.rsqrt(jnp.mean(centred * centred, axis=-1, keepdims=True) + epsilon)
    return mean, inverse, centred * inverse


def pack_kernel(count, cap, stamps, me_ref, meta_ref, *refs):
    arrays, outs = refs[: len(stamps)], refs[len(stamps) :]
    picks = routing(me_ref[0], meta_ref, count, cap)
    whole = jnp.concatenate(picks, axis=0).astype(bf16)
    for index, stamped in enumerate(stamps):
        rows = dot(whole, arrays[index][...]).astype(bf16)
        width = rows.shape[1]
        for k in range(count):
            out = outs[index * count + k]
            out[:, :width] = rows[k * cap : (k + 1) * cap]
            if stamped:
                marks = picks[k] * (meta_ref[2:3, :] + 1).astype(f32)
                column = jnp.sum(marks, axis=1, keepdims=True)
                out[:, width:] = jnp.broadcast_to(column, (cap, LANES)).astype(bf16)


def pack(me, meta, arrays, stamps, count, cap):
    width = arrays[0].shape[1]
    outs = [
        jax.ShapeDtypeStruct((cap, width + LANES if stamped else width), bf16)
        for stamped in stamps
        for _ in range(count)
    ]
    outs = pl.pallas_call(
        functools.partial(pack_kernel, count, cap, stamps),
        out_shape=outs,
        in_specs=[SMEM] + [VMEM] * (1 + len(arrays)),
        out_specs=[VMEM] * len(outs),
        compiler_params=params(24),
        cost_estimate=cost(4e9, 2e6),
        name="pack",
    )(me, meta, *arrays)
    return [outs[i * count : (i + 1) * count] for i in range(len(arrays))]


def forward_kernel(count, me_ref, *refs):
    blocks, refs = refs[:count], refs[count:]
    table_ref, router_ref, gate_a, up_a, gate_b, up_b = refs[:6]
    mod_ref, stats_ref, act_ref, fac_ref, hid_ref = refs[6:11]
    weights, sems = refs[11:15], refs[15]
    copies = [
        pltpu.make_async_copy(source, target, sems.at[i])
        for i, (source, target) in enumerate(zip((gate_a, up_a, gate_b, up_b), weights))
    ]
    for copy in copies:
        copy.start()
    cap, width = blocks[0].shape[0], mod_ref.shape[1]
    half = weights[0].shape[1]
    conditions = table_ref.shape[1]
    shift_parts, scale_parts = split3(table_ref[0]), split3(table_ref[1])
    router_row = own_row(me_ref[0], router_ref)
    lane = lax.broadcasted_iota(jnp.int32, (cap, LANES), 1)
    for k in range(count):
        mean, inverse, normed = normalize(blocks[k][:, :width].astype(f32))
        mark = blocks[k][:, width : width + 1].astype(f32)
        pick = pick3(mark, conditions)
        rows = (normed * (1.0 + dot(pick, scale_parts)) + dot(pick, shift_parts)).astype(bf16)
        mod_ref[k * cap : (k + 1) * cap, :] = rows
        logit = jnp.sum(rows.astype(f32) * router_row, axis=1, keepdims=True)
        prob = jax.nn.sigmoid(logit)
        stats_ref[k * cap : (k + 1) * cap, :] = jnp.where(
            lane == 0, mean, jnp.where(lane == 1, inverse, jnp.where(lane == 2, prob, mark))
        )
    for part in range(2):
        copies[2 * part].wait()
        pre_gate = dot(mod_ref[...], weights[2 * part][...])
        copies[2 * part + 1].wait()
        pre_up = dot(mod_ref[...], weights[2 * part + 1][...])
        sig = jax.nn.sigmoid(pre_gate)
        active = pre_gate * sig
        columns = slice(part * half, (part + 1) * half)
        act_ref[:, columns] = active
        fac_ref[:, columns] = pre_up * sig * (1.0 + pre_gate * (1.0 - sig))
        hid_ref[:, columns] = (active * pre_up).astype(bf16)


def forward(me, blocks, table, router, gates, ups):
    count, cap, wide = len(blocks), *blocks[0].shape
    width, half = gates[0].shape
    rows = count * cap
    return pl.pallas_call(
        functools.partial(forward_kernel, count),
        out_shape=[
            jax.ShapeDtypeStruct((rows, width), bf16),
            jax.ShapeDtypeStruct((rows, LANES), f32),
            jax.ShapeDtypeStruct((rows, 2 * half), f32),
            jax.ShapeDtypeStruct((rows, 2 * half), f32),
            jax.ShapeDtypeStruct((rows, 2 * half), bf16),
        ],
        in_specs=[SMEM] + [VMEM] * (count + 2) + [ANY] * 4,
        out_specs=[VMEM] * 5,
        scratch_shapes=[pltpu.VMEM((width, half), bf16)] * 4 + [pltpu.SemaphoreType.DMA((4,))],
        compiler_params=params(40),
        cost_estimate=cost(8 * rows * width * half, 4 * 2 * width * half + rows * 12000),
        name="expert_in",
    )(me, *blocks, table, router, gates[0], ups[0], gates[1], ups[1])


def backward_kernel(count, me_ref, *refs):
    blocks, refs = refs[:count], refs[count:]
    table_ref, router_ref, stats_ref, act_ref, fac_ref, hid_ref = refs[:6]
    sources, refs = refs[6:12], refs[12:]
    backs, refs = refs[:count], refs[count:]
    og_ref, gg_ref, ug_ref, lg_ref = refs[:4]
    up_ref, weights, sems = refs[4], refs[5:11], refs[11]
    copies = [
        pltpu.make_async_copy(source, target, sems.at[i])
        for i, (source, target) in enumerate(zip(sources, weights))
    ]
    for copy in copies:
        copy.start()
    cap, width = blocks[0].shape
    half = weights[0].shape[1]
    conditions = table_ref.shape[1]
    gate_parts = split3(table_ref[2])
    prob = stats_ref[:, 2:3]
    for k in range(count):
        rows = slice(k * cap, (k + 1) * cap)
        pick = pick3(stats_ref[rows, 3:4], conditions)
        upstream = (dot(pick, gate_parts) * blocks[k][...].astype(f32)).astype(bf16)
        up_ref[rows, :] = upstream
        og_ref[rows, :] = (stats_ref[rows, 2:3] * upstream.astype(f32)).astype(bf16)
    prob_grad = jnp.zeros((count * cap, 1), f32)
    total = None
    for part in range(2):
        down, gate, up = (weights[3 * part + i] for i in range(3))
        columns = slice(part * half, (part + 1) * half)
        copies[3 * part].wait()
        raw = dot(up_ref[...], down[...])
        prob_grad += jnp.sum(hid_ref[:, columns].astype(f32) * raw, axis=1, keepdims=True)
        hidden_grad = prob * raw
        gate_grad = (hidden_grad * fac_ref[:, columns]).astype(bf16)
        up_grad = (hidden_grad * act_ref[:, columns]).astype(bf16)
        gg_ref[:, columns] = gate_grad
        ug_ref[:, columns] = up_grad
        copies[3 * part + 1].wait()
        term = dot(gate_grad, gate[...], ((1,), (1,)))
        copies[3 * part + 2].wait()
        term += dot(up_grad, up[...], ((1,), (1,)))
        total = term if total is None else total + term
    logit_grad = prob_grad * prob * (1.0 - prob)
    lg_ref[...] = jnp.broadcast_to(logit_grad, lg_ref.shape)
    router_row = own_row(me_ref[0], router_ref)
    total += logit_grad * router_row
    for k in range(count):
        backs[k][...] = total[k * cap : (k + 1) * cap].astype(bf16)


def backward(me, blocks, table, router, stats, act, fac, hid, weights):
    count, cap, width = len(blocks), *blocks[0].shape
    half = weights[0].shape[1]
    rows = count * cap
    outs = pl.pallas_call(
        functools.partial(backward_kernel, count),
        out_shape=[jax.ShapeDtypeStruct((cap, width), bf16)] * count
        + [
            jax.ShapeDtypeStruct((rows, width), bf16),
            jax.ShapeDtypeStruct((rows, 2 * half), bf16),
            jax.ShapeDtypeStruct((rows, 2 * half), bf16),
            jax.ShapeDtypeStruct((rows, LANES), f32),
        ],
        in_specs=[SMEM] + [VMEM] * (count + 6) + [ANY] * 6,
        out_specs=[VMEM] * (count + 4),
        scratch_shapes=[pltpu.VMEM((rows, width), bf16)]
        + [pltpu.VMEM((width, half), bf16)] * 6
        + [pltpu.SemaphoreType.DMA((6,))],
        compiler_params=params(40),
        cost_estimate=cost(12 * rows * width * half, 6 * 2 * width * half + rows * 16000),
        name="expert_back",
    )(me, *blocks, table, router, stats, act, fac, hid, *weights)
    return outs[:count], *outs[count:]


def sums_kernel(count, tall, me_ref, *refs):
    blocks, refs = refs[: 2 * count], refs[2 * count :]
    backs, refs = refs[: 2 * count], refs[2 * count :]
    mods, refs = refs[:2], refs[2:]
    stats, refs = refs[:2], refs[2:]
    lgs, refs = refs[:2], refs[2:]
    meta_ref, cot_ref, mix_ref, out_ref = refs
    cap, width = backs[0].shape
    conditions, experts = tall
    zero = ((0,), (0,))
    shift_sum = jnp.zeros((conditions, width), f32)
    scale_sum = jnp.zeros((conditions, width), f32)
    router_sum = jnp.zeros((1, width), f32)
    for index in range(2 * count):
        q, k = divmod(index, count)
        rows = slice(k * cap, (k + 1) * cap)
        lane = lax.broadcasted_iota(jnp.int32, (cap, conditions), 1)
        mark = stats[q][rows, 3:4].astype(jnp.int32)
        pick = (lane + 1 == mark).astype(f32).astype(bf16)
        back = backs[index][...]
        mean, inverse = stats[q][rows, 0:1], stats[q][rows, 1:2]
        normed = (blocks[index][:, :width].astype(f32) - mean) * inverse
        product = back.astype(f32) * normed
        high = product.astype(bf16)
        low = (product - high.astype(f32)).astype(bf16)
        shift_sum += dot(pick, back, zero)
        scale_sum += dot(pick, high, zero) + dot(pick, low, zero)
        weighted = lgs[q][rows, 0:1] * mods[q][rows, :].astype(f32)
        router_sum += jnp.sum(weighted, axis=0, keepdims=True)
    toks = cot_ref.shape[0]
    wanted = lax.broadcasted_iota(jnp.int32, (conditions, toks), 0)
    pick = (meta_ref[2:3, :] == wanted).astype(f32).astype(bf16)
    product = cot_ref[...].astype(f32) * mix_ref[...].astype(f32)
    high = product.astype(bf16)
    low = (product - high.astype(f32)).astype(bf16)
    out_ref[0:conditions, :] = shift_sum
    out_ref[conditions : 2 * conditions, :] = scale_sum
    out_ref[2 * conditions : 3 * conditions, :] = dot(pick, high) + dot(pick, low)
    place = lax.broadcasted_iota(jnp.int32, (out_ref.shape[0] - 3 * conditions, width), 0)
    out_ref[3 * conditions :, :] = jnp.where(place == me_ref[0], router_sum, 0.0)


def sums(me, blocks, backs, mods, stats, lgs, meta, cot, mix, conditions, experts):
    height = -(-(3 * conditions + experts) // 128) * 128
    width = cot.shape[1]
    count = len(blocks) // 2
    return pl.pallas_call(
        functools.partial(sums_kernel, count, (conditions, experts)),
        out_shape=jax.ShapeDtypeStruct((height, width), f32),
        in_specs=[SMEM] + [VMEM] * (4 * count + 9),
        out_specs=VMEM,
        compiler_params=params(40),
        cost_estimate=cost(4e9, 8e6),
        name="table_sums",
    )(me, *blocks, *backs, *mods, *stats, *lgs, meta, cot, mix)


def grads_kernel(*refs):
    mods, ogs, ggs, ugs, hids = (refs[2 * i : 2 * i + 2] for i in range(5))
    mine_ref, other_ref = refs[10:]
    half = mine_ref.shape[2]
    zero = ((0,), (0,))
    for index, (left, right) in enumerate(((mods, ggs), (mods, ugs), (ogs, hids))):
        total = dot(left[0][...], right[0][...], zero) + dot(left[1][...], right[1][...], zero)
        mine_ref[index] = total[:, :half].astype(bf16)
        other_ref[index] = total[:, half:].astype(bf16)


def grads(mods, ogs, ggs, ugs, hids):
    rows, width = mods[0].shape
    full = ggs[0].shape[1]
    step = 256
    left = pl.BlockSpec((rows, step), lambda i: (0, i))
    right = pl.BlockSpec((rows, full), lambda i: (0, 0))
    out = pl.BlockSpec((3, step, full // 2), lambda i: (0, i, 0))
    return pl.pallas_call(
        grads_kernel,
        grid=(width // step,),
        out_shape=[jax.ShapeDtypeStruct((3, width, full // 2), bf16)] * 2,
        in_specs=[left] * 4 + [right] * 6,
        out_specs=[out] * 2,
        compiler_params=params(40),
        cost_estimate=cost(12 * rows * width * full, 12e6),
        name="weight_grads",
    )(*mods, *ogs, *ggs, *ugs, *hids)


def final_kernel(count, cap, me_ref, meta_ref, stamp_ref, tok_ref, cot_ref, table_ref, *refs):
    backs, out_ref = refs[:count], refs[count]
    picks = jnp.concatenate(routing(me_ref[0], meta_ref, count, cap), axis=0).astype(bf16)
    rows = jnp.concatenate([back[...] for back in backs], axis=0)
    mod_grad = dot(picks, rows, ((0,), (0,)))
    conditions = table_ref.shape[1]
    _, inverse, normed = normalize(tok_ref[...].astype(f32))
    pick = pick3((stamp_ref[:, 0:1] + 1).astype(f32), conditions)
    d_normed = mod_grad * (1.0 + dot(pick, split3(table_ref[1])))
    d_input = inverse * (
        d_normed
        - jnp.mean(d_normed, axis=-1, keepdims=True)
        - normed * jnp.mean(d_normed * normed, axis=-1, keepdims=True)
    )
    out_ref[...] = (cot_ref[...].astype(f32) + d_input).astype(bf16)


def final(me, meta, stamp_column, tokens, cot, table, backs, cap):
    count = len(backs)
    return pl.pallas_call(
        functools.partial(final_kernel, count, cap),
        out_shape=jax.ShapeDtypeStruct(tokens.shape, bf16),
        in_specs=[SMEM] + [VMEM] * (5 + count),
        out_specs=VMEM,
        compiler_params=params(40),
        cost_estimate=cost(1e9, 4e6),
        name="final",
    )(me, meta, stamp_column, tokens, cot, table, *backs)


def reduce_table(table, axes):
    steps = []
    for name, size in axes:
        bit = 1
        while bit < size:
            steps.append((name, size, bit))
            bit *= 2
    for name, size, bit in steps:
        pairs = [(i, i ^ bit) for i in range(size)]
        high = (lax.axis_index(name) & bit) != 0
        rows = table.shape[0] // 2
        low_half, high_half = table[:rows], table[rows:]
        away = jnp.where(high, low_half, high_half).astype(bf16)
        table = jnp.where(high, high_half, low_half)
        table = table + lax.ppermute(away, name, pairs).astype(f32)
    table = table.astype(bf16)
    for name, size, bit in reversed(steps):
        pairs = [(i, i ^ bit) for i in range(size)]
        high = (lax.axis_index(name) & bit) != 0
        other = lax.ppermute(table, name, pairs)
        table = jnp.concatenate(
            [jnp.where(high, other, table), jnp.where(high, table, other)], axis=0
        )
    return table.astype(f32)


def local(experts_axis, dp_axis, tokens, cotangent, mixture, stamp, expert_ids, modulation, router, w_gate, w_up, w_down):
    toks, width = tokens.shape
    conditions = modulation.shape[1]
    experts = experts_axis
    cap = min(toks, 4 * toks // experts)
    half = experts // 2
    me = lax.axis_index("expert").astype(jnp.int32)[None]

    def hop(array, k):
        return lax.ppermute(array, "expert", [(e, e ^ k) for e in range(experts)])

    def swap(array):
        return lax.ppermute(array, "dp", [(i, dp_axis - 1 - i) for i in range(dp_axis)])

    meta = jnp.concatenate(
        [expert_ids.T, stamp[None], jnp.zeros((5, toks), jnp.int32)], axis=0
    )
    far_meta = hop(meta, half)
    far_tokens = hop(tokens, half)
    far_cot = hop(cotangent, half)
    (near_rows, near_cots) = pack(me, meta, [tokens, cotangent], (True, False), half, cap)
    near_rows = [near_rows[0]] + [hop(near_rows[k], k) for k in range(1, half)]
    near_cots = [near_cots[0]] + [hop(near_cots[k], k) for k in range(1, half)]
    gates = [w_gate[0], swap(w_gate[0])]
    ups = [w_up[0], swap(w_up[0])]
    downs = [w_down[0], swap(w_down[0])]
    weights = [downs[0], gates[0], ups[0], downs[1], gates[1], ups[1]]
    (far_rows,) = pack(me, far_meta, [far_tokens], (True,), half, cap)
    far_rows = [far_rows[0]] + [hop(far_rows[k], k) for k in range(1, half)]
    (far_cots,) = pack(me, far_meta, [far_cot], (False,), half, cap)
    far_cots = [far_cots[0]] + [hop(far_cots[k], k) for k in range(1, half)]

    mods, stats, backs, ogs, ggs, ugs, lgs, hids = ([] for _ in range(8))
    for rows, cots in ((near_rows, near_cots), (far_rows, far_cots)):
        mod, stat, act, fac, hid = forward(me, rows, modulation, router, gates, ups)
        back, og, gg, ug, lg = backward(
            me, cots, modulation, router, stat, act, fac, hid, weights
        )
        for group, item in zip(
            (mods, stats, ogs, ggs, ugs, lgs, hids), (mod, stat, og, gg, ug, lg, hid)
        ):
            group.append(item)
        backs += list(back)
    returned = [backs[0]] + [hop(backs[k], k) for k in range(1, experts)]
    table = sums(
        me, list(near_rows) + list(far_rows), backs, mods, stats, lgs,
        meta, cotangent, mixture, conditions, experts,
    )
    mine, other = grads(mods, ogs, ggs, ugs, hids)
    other = swap(other)
    table = reduce_table(table, (("dp", dp_axis), ("expert", experts)))
    total = (mine.astype(f32) + other.astype(f32)).astype(bf16)
    d_tokens = final(me, meta, stamp[:, None], tokens, cotangent, modulation, returned, cap)
    d_modulation = table[: 3 * conditions].reshape(3, conditions, width)
    d_router = table[3 * conditions : 3 * conditions + experts]
    return (d_tokens, total[0:1], total[1:2], total[2:3], d_router, d_modulation)


def solution(mesh):
    return jax.shard_map(
        functools.partial(local, mesh.shape["expert"], mesh.shape["dp"]),
        mesh=mesh,
        in_specs=(
            P(("groups", "expert", "dp"), None),
            P(("groups", "expert", "dp"), None),
            P(("groups", "expert", "dp"), None),
            P(("groups", "expert", "dp")),
            P(("groups", "expert", "dp"), None),
            P(),
            P(),
            P("expert", None, "dp"),
            P("expert", None, "dp"),
            P("expert", None, "dp"),
        ),
        out_specs=(
            P(("groups", "expert", "dp"), None),
            P(("groups", "expert"), None, "dp"),
            P(("groups", "expert"), None, "dp"),
            P(("groups", "expert"), None, "dp"),
            P("groups", None),
            P(None, "groups", None),
        ),
        check_vma=False,
    )
```

```python
import functools

import jax
import jax.numpy as jnp
from jax import lax
from jax.experimental import pallas as pl
from jax.experimental.pallas import tpu as pltpu
from jax.sharding import PartitionSpec as P

epsilon = 1e-06
f32 = jnp.float32
bf16 = jnp.bfloat16
LANES = 128
VMEM = pl.BlockSpec(memory_space=pltpu.VMEM)
SMEM = pl.BlockSpec(memory_space=pltpu.SMEM)


def params(mib):
    return pltpu.CompilerParams(vmem_limit_bytes=mib * 1024 * 1024)


def cost(flops, moved):
    return pl.CostEstimate(flops=int(flops), bytes_accessed=int(moved), transcendentals=0)


def dot(a, b, dims=((1,), (0,))):
    return lax.dot_general(a, b, (dims, ((), ())), preferred_element_type=f32)


def routing(base, flip, meta_ref, count, cap):
    toks = meta_ref.shape[1]
    height = max(8, count)
    wanted = base + jnp.bitwise_xor(
        flip, lax.broadcasted_iota(jnp.int32, (height, toks), 0)
    )
    member = jnp.logical_or(meta_ref[0:1, :] == wanted, meta_ref[1:2, :] == wanted)
    earlier = lax.broadcasted_iota(jnp.int32, (toks, toks), 0) < lax.broadcasted_iota(
        jnp.int32, (toks, toks), 1
    )
    slots = dot(member.astype(f32).astype(bf16), earlier.astype(f32).astype(bf16))
    slots = jnp.where(member, slots, -1.0).astype(jnp.int32)
    place = lax.broadcasted_iota(jnp.int32, (cap, toks), 0)
    picks = [(slots[k : k + 1, :] == place).astype(f32) for k in range(count)]
    return jnp.concatenate(picks, axis=0)


def split3(table):
    high = table.astype(bf16)
    rest = table - high.astype(f32)
    middle = rest.astype(bf16)
    low = (rest - middle.astype(f32)).astype(bf16)
    return jnp.concatenate([high, middle, low], axis=0)


def pick3(column, conditions):
    lane = lax.broadcasted_iota(jnp.int32, (column.shape[0], 3 * conditions), 1)
    return (lax.rem(lane, conditions) + 1 == column.astype(jnp.int32)).astype(f32).astype(bf16)


def own_row(me, router_ref):
    table = router_ref[...].astype(f32)
    place = lax.broadcasted_iota(jnp.int32, table.shape, 0)
    return jnp.sum(jnp.where(place == me, table, 0.0), axis=0, keepdims=True)


def normalize(values):
    mean = jnp.mean(values, axis=-1, keepdims=True)
    centred = values - mean
    inverse = lax.rsqrt(jnp.mean(centred * centred, axis=-1, keepdims=True) + epsilon)
    return mean, inverse, centred * inverse


def piece(refs, start, size, columns):
    height = refs[0].shape[0]
    if size <= height:
        block, row = divmod(start, height)
        return refs[block][row : row + size, columns]
    parts = [refs[start // height + i][:, columns] for i in range(size // height)]
    return jnp.concatenate(parts, axis=0)


def put(refs, start, values, columns):
    height = refs[0].shape[0]
    size = values.shape[0]
    if size <= height:
        block, row = divmod(start, height)
        refs[block][row : row + size, columns] = values
    else:
        for i in range(size // height):
            refs[start // height + i][:, columns] = values[i * height : (i + 1) * height]


def pack_kernel(count, cap, number, flipped, stamped, me_ref, meta_ref, *refs):
    arrays, outs = refs[:number], refs[number:]
    flip = me_ref[0] - me_ref[1] if flipped else 0
    picks = routing(me_ref[1], flip, meta_ref, count, cap)
    whole = picks.astype(bf16)
    total = count * cap
    width = arrays[0].shape[1]
    put(outs, 0, dot(whole, arrays[0][...]).astype(bf16), slice(0, width))
    at = width
    if stamped:
        column = jnp.sum(picks * (meta_ref[2:3, :] + 1).astype(f32), axis=1, keepdims=True)
        put(outs, 0, jnp.broadcast_to(column, (total, LANES)).astype(bf16), slice(at, at + LANES))
        at += LANES
    for array in arrays[1:]:
        put(outs, 0, dot(whole, array[...]).astype(bf16), slice(at, at + width))
        at += width


def pack(me, meta, arrays, stamped, flipped, count, cap):
    width = arrays[0].shape[1] * len(arrays) + (LANES if stamped else 0)
    shape = (cap, width) if flipped else (count * cap, width)
    number = count if flipped else 1
    return pl.pallas_call(
        functools.partial(pack_kernel, count, cap, len(arrays), flipped, stamped),
        out_shape=[jax.ShapeDtypeStruct(shape, bf16)] * number,
        in_specs=[SMEM] + [VMEM] * (1 + len(arrays)),
        out_specs=[VMEM] * number,
        compiler_params=params(8),
        cost_estimate=cost(1e9, 4e6),
        name="pack",
    )(me, meta, *arrays)


def late_views(late_ref, width, full):
    edges = [0, width, 2 * width, 2 * width + full, 2 * width + 2 * full, 2 * width + 3 * full]
    return [late_ref.at[:, low:high] for low, high in zip(edges, edges[1:])]


def forward_body(me_ref, ins, table_ref, router_ref, gate_ref, up_ref, mod_ref, stats_ref, act_ref, fac_ref, hid_ref):
    count, width = mod_ref.shape
    full = gate_ref.shape[1]
    conditions = table_ref.shape[1]
    chunk = 64
    shift_parts, scale_parts = split3(table_ref[0]), split3(table_ref[1])
    router_row = own_row(me_ref[0], router_ref)
    lane = lax.broadcasted_iota(jnp.int32, (chunk, LANES), 1)
    for start in range(0, count, chunk):
        part = slice(start, start + chunk)
        mean, inverse, normed = normalize(piece(ins, start, chunk, slice(0, width)).astype(f32))
        mark = piece(ins, start, chunk, slice(width, width + 1)).astype(f32)
        pick = pick3(mark, conditions)
        rows = (normed * (1.0 + dot(pick, scale_parts)) + dot(pick, shift_parts)).astype(bf16)
        mod_ref[part, :] = rows
        logit = jnp.sum(rows.astype(f32) * router_row, axis=1, keepdims=True)
        prob = jax.nn.sigmoid(logit)
        stats_ref[part, :] = jnp.where(
            lane == 0, mean, jnp.where(lane == 1, inverse, jnp.where(lane == 2, prob, mark))
        )
    step = 256
    for start in range(0, full, step):
        columns = slice(start, start + step)
        pre_gate = dot(mod_ref[...], gate_ref[:, columns])
        pre_up = dot(mod_ref[...], up_ref[:, columns])
        sig = jax.nn.sigmoid(pre_gate)
        active = pre_gate * sig
        act_ref[:, columns] = active
        fac_ref[:, columns] = pre_up * sig * (1.0 + pre_gate * (1.0 - sig))
        hid_ref[:, columns] = (active * pre_up).astype(bf16)


def backward_body(offset, me_ref, cots, table_ref, router_ref, stats_ref, act_ref, fac_ref, hid_ref, down_ref, gate_ref, up_ref, backs, og_ref, gg_ref, ug_ref, lg_ref, ups_ref):
    count, width = og_ref.shape
    full = gate_ref.shape[1]
    conditions = table_ref.shape[1]
    gate_parts = split3(table_ref[2])
    prob = stats_ref[:, 2:3]
    chunk = 64
    for start in range(0, count, chunk):
        part = slice(start, start + chunk)
        pick = pick3(stats_ref[part, 3:4], conditions)
        cot = piece(cots, start, chunk, slice(offset, offset + width)).astype(f32)
        upstream = (dot(pick, gate_parts) * cot).astype(bf16)
        ups_ref[part, :] = upstream
        og_ref[part, :] = (stats_ref[part, 2:3] * upstream.astype(f32)).astype(bf16)
    prob_grad = jnp.zeros((count, 1), f32)
    step = 256
    for start in range(0, full, step):
        columns = slice(start, start + step)
        raw = dot(ups_ref[...], down_ref[:, columns])
        prob_grad += jnp.sum(hid_ref[:, columns].astype(f32) * raw, axis=1, keepdims=True)
        hidden_grad = prob * raw
        gg_ref[:, columns] = (hidden_grad * fac_ref[:, columns]).astype(bf16)
        ug_ref[:, columns] = (hidden_grad * act_ref[:, columns]).astype(bf16)
    logit_grad = prob_grad * prob * (1.0 - prob)
    lane = lax.broadcasted_iota(jnp.int32, stats_ref.shape, 1)
    lg_ref[...] = jnp.where(lane == 4, logit_grad, stats_ref[...])
    router_row = own_row(me_ref[0], router_ref)
    for start in range(0, width, step):
        part = slice(start, start + step)
        total = dot(gg_ref[...], gate_ref[part, :], ((1,), (1,)))
        total += dot(ug_ref[...], up_ref[part, :], ((1,), (1,)))
        put(backs, 0, (total + logit_grad * router_row[:, part]).astype(bf16), part)


def forward_kernel(number, me_ref, *refs):
    forward_body(me_ref, refs[:number], *refs[number:])


def forward(me, blocks, table, router, gate, up):
    count = sum(block.shape[0] for block in blocks)
    width, full = gate.shape
    wide = jax.ShapeDtypeStruct((count, full), f32)
    return pl.pallas_call(
        functools.partial(forward_kernel, len(blocks)),
        out_shape=[
            jax.ShapeDtypeStruct((count, width), bf16),
            jax.ShapeDtypeStruct((count, LANES), f32),
            wide,
            wide,
            jax.ShapeDtypeStruct((count, full), bf16),
        ],
        in_specs=[SMEM] + [VMEM] * (len(blocks) + 4),
        out_specs=[VMEM] * 5,
        compiler_params=params(12),
        cost_estimate=cost(4 * count * width * full, 4 * width * full + count * 12000),
        name="expert_in",
    )(me, *blocks, table, router, gate, up)


def backward_shapes(blocks, width, full):
    count = sum(block.shape[0] for block in blocks)
    return [jax.ShapeDtypeStruct((block.shape[0], width), bf16) for block in blocks] + [
        jax.ShapeDtypeStruct((count, 2 * width + 3 * full), bf16),
        jax.ShapeDtypeStruct((count, LANES), f32),
    ]


def backward_kernel(number, me_ref, *refs):
    cots, refs = refs[:number], refs[number:]
    table_ref, router_ref, seen_ref, stats_ref, act_ref, fac_ref, hid_ref, down_ref, gate_ref, up_ref = refs[:10]
    backs, (late_ref, lg_ref, ups_ref) = refs[10 : 10 + number], refs[10 + number :]
    mod, og, gg, ug, hid = late_views(late_ref, *gate_ref.shape)
    backward_body(0, me_ref, cots, table_ref, router_ref, stats_ref, act_ref, fac_ref, hid_ref, down_ref, gate_ref, up_ref, backs, og, gg, ug, lg_ref, ups_ref)
    mod[...] = seen_ref[...]
    hid[...] = hid_ref[...]


def backward(me, blocks, table, router, mod, stats, act, fac, hid, down, gate, up):
    count = sum(block.shape[0] for block in blocks)
    width, full = gate.shape
    number = len(blocks)
    outs = pl.pallas_call(
        functools.partial(backward_kernel, number),
        out_shape=backward_shapes(blocks, width, full),
        in_specs=[SMEM] + [VMEM] * (number + 10),
        out_specs=[VMEM] * (number + 2),
        scratch_shapes=[pltpu.VMEM((count, width), bf16)],
        compiler_params=params(12),
        cost_estimate=cost(6 * count * width * full, 6 * width * full + count * 16000),
        name="expert_back",
    )(me, *blocks, table, router, mod, stats, act, fac, hid, down, gate, up)
    return outs[:number], *outs[number:]


def whole_kernel(number, me_ref, *refs):
    blocks, refs = refs[:number], refs[number:]
    table_ref, router_ref, down_ref, gate_ref, up_ref = refs[:5]
    backs, refs = refs[5 : 5 + number], refs[5 + number :]
    late_ref, lg_ref, stats_ref, act_ref, fac_ref, ups_ref = refs
    mod, og, gg, ug, hid = late_views(late_ref, *gate_ref.shape)
    forward_body(me_ref, blocks, table_ref, router_ref, gate_ref, up_ref, mod, stats_ref, act_ref, fac_ref, hid)
    backward_body(mod.shape[1] + LANES, me_ref, blocks, table_ref, router_ref, stats_ref, act_ref, fac_ref, hid, down_ref, gate_ref, up_ref, backs, og, gg, ug, lg_ref, ups_ref)


def whole(me, blocks, table, router, down, gate, up):
    count = sum(block.shape[0] for block in blocks)
    width, full = gate.shape
    number = len(blocks)
    outs = pl.pallas_call(
        functools.partial(whole_kernel, number),
        out_shape=backward_shapes(blocks, width, full),
        in_specs=[SMEM] + [VMEM] * (number + 5),
        out_specs=[VMEM] * (number + 2),
        scratch_shapes=[pltpu.VMEM((count, LANES), f32)]
        + [pltpu.VMEM((count, full), f32)] * 2
        + [pltpu.VMEM((count, width), bf16)],
        compiler_params=params(16),
        cost_estimate=cost(10 * count * width * full, 6 * width * full + count * 16000),
        name="expert_whole",
    )(me, *blocks, table, router, down, gate, up)
    return outs[:number], *outs[number:]


def sums_kernel(numbers, tall, me_ref, *refs):
    rows, backs = [], []
    for group in (rows, backs):
        for number in numbers:
            group.append(refs[:number])
            refs = refs[number:]
    lates, stats = refs[:2], refs[2:4]
    meta_ref, cot_ref, mix_ref, out_ref = refs[4:]
    count, width = lates[0].shape[0], cot_ref.shape[1]
    conditions, experts = tall
    zero = ((0,), (0,))
    shift_sum = jnp.zeros((conditions, width), f32)
    scale_sum = jnp.zeros((conditions, width), f32)
    router_sum = jnp.zeros((1, width), f32)
    chunk = 128
    for q in range(2):
        for start in range(0, count, chunk):
            part = slice(start, start + chunk)
            lane = lax.broadcasted_iota(jnp.int32, (chunk, conditions), 1)
            mark = stats[q][part, 3:4].astype(jnp.int32)
            pick = (lane + 1 == mark).astype(f32).astype(bf16)
            back = piece(backs[q], start, chunk, slice(0, width))
            mean, inverse = stats[q][part, 0:1], stats[q][part, 1:2]
            values = piece(rows[q], start, chunk, slice(0, width)).astype(f32)
            normed = (values - mean) * inverse
            product = back.astype(f32) * normed
            high = product.astype(bf16)
            low = (product - high.astype(f32)).astype(bf16)
            shift_sum += dot(pick, back, zero)
            scale_sum += dot(pick, high, zero) + dot(pick, low, zero)
            weighted = stats[q][part, 4:5] * lates[q][part, :width].astype(f32)
            router_sum += jnp.sum(weighted, axis=0, keepdims=True)
    toks = cot_ref.shape[0]
    wanted = lax.broadcasted_iota(jnp.int32, (conditions, toks), 0)
    pick = (meta_ref[2:3, :] == wanted).astype(f32).astype(bf16)
    product = cot_ref[...].astype(f32) * mix_ref[...].astype(f32)
    high = product.astype(bf16)
    low = (product - high.astype(f32)).astype(bf16)
    out_ref[0:conditions, :] = shift_sum
    out_ref[conditions : 2 * conditions, :] = scale_sum
    out_ref[2 * conditions : 3 * conditions, :] = dot(pick, high) + dot(pick, low)
    place = lax.broadcasted_iota(jnp.int32, (out_ref.shape[0] - 3 * conditions, width), 0)
    out_ref[3 * conditions :, :] = jnp.where(place == me_ref[0], router_sum, 0.0)


def sums(me, rows, backs, lates, stats, meta, cot, mix, conditions, experts):
    numbers = [len(blocks) for blocks in rows]
    height = -(-(3 * conditions + experts) // 128) * 128
    width = cot.shape[1]
    return pl.pallas_call(
        functools.partial(sums_kernel, numbers, (conditions, experts)),
        out_shape=jax.ShapeDtypeStruct((height, width), f32),
        in_specs=[SMEM] + [VMEM] * (2 * sum(numbers) + 7),
        out_specs=VMEM,
        compiler_params=params(12),
        cost_estimate=cost(1e6, 1e4),
        name="table_sums",
    )(me, *rows[0], *rows[1], *backs[0], *backs[1], *lates, *stats, meta, cot, mix)


def grads_kernel(me_ref, near_ref, far_ref, *outs):
    width, half = outs[0].shape
    other_ref = outs[3]
    zero = ((0,), (0,))
    second = me_ref[2] != 0
    step = 256
    near, far = (late_views(ref, width, 2 * half) for ref in (near_ref, far_ref))
    for start in range(0, width, step):
        part = slice(start, start + step)
        for index, (left, right) in enumerate(((0, 2), (0, 3), (1, 4))):
            total = dot(near[left][:, part], near[right][...], zero)
            total += dot(far[left][:, part], far[right][...], zero)
            low, high = total[:, :half], total[:, half:]
            outs[index][part, :] = jnp.where(second, high, low).astype(bf16)
            other_ref[index, part, :] = jnp.where(second, low, high).astype(bf16)


def grads(me, lates, width, full):
    outs = pl.pallas_call(
        grads_kernel,
        out_shape=[jax.ShapeDtypeStruct((width, full // 2), bf16)] * 3
        + [jax.ShapeDtypeStruct((3, width, full // 2), bf16)],
        in_specs=[SMEM] + [VMEM] * 2,
        out_specs=[VMEM] * 4,
        compiler_params=params(12),
        cost_estimate=cost(1e6, 1e4),
        name="weight_grads",
    )(me, *lates)
    return outs[:3], outs[3]


def merge_kernel(count, cap, me_ref, meta_ref, *refs):
    picks = routing(me_ref[1], me_ref[0] - me_ref[1], meta_ref, count, cap).astype(bf16)
    rows = piece(refs[:-1], 0, count * cap, slice(None))
    refs[-1][...] = dot(picks, rows, ((0,), (0,))).astype(bf16)


def merge(me, meta, backs, cap):
    return pl.pallas_call(
        functools.partial(merge_kernel, len(backs), cap),
        out_shape=jax.ShapeDtypeStruct((meta.shape[1], backs[0].shape[1]), bf16),
        in_specs=[SMEM] + [VMEM] * (1 + len(backs)),
        out_specs=VMEM,
        compiler_params=params(8),
        cost_estimate=cost(1e9, 2e6),
        name="merge",
    )(me, meta, *backs)


def final_kernel(count, cap, me_ref, meta_ref, stamp_ref, tok_ref, cot_ref, table_ref, near_ref, far_ref, out_ref):
    picks = routing(me_ref[1], 0, meta_ref, count, cap).astype(bf16)
    mod_grad = dot(picks, near_ref[...], ((0,), (0,))) + far_ref[...].astype(f32)
    conditions = table_ref.shape[1]
    _, inverse, normed = normalize(tok_ref[...].astype(f32))
    pick = pick3((stamp_ref[:, 0:1] + 1).astype(f32), conditions)
    d_normed = mod_grad * (1.0 + dot(pick, split3(table_ref[1])))
    d_input = inverse * (
        d_normed
        - jnp.mean(d_normed, axis=-1, keepdims=True)
        - normed * jnp.mean(d_normed * normed, axis=-1, keepdims=True)
    )
    out_ref[...] = (cot_ref[...].astype(f32) + d_input).astype(bf16)


def final(me, meta, stamp_column, tokens, cot, table, near, far, count, cap):
    return pl.pallas_call(
        functools.partial(final_kernel, count, cap),
        out_shape=jax.ShapeDtypeStruct(tokens.shape, bf16),
        in_specs=[SMEM] + [VMEM] * 7,
        out_specs=VMEM,
        compiler_params=params(12),
        cost_estimate=cost(1e9, 4e6),
        name="final",
    )(me, meta, stamp_column, tokens, cot, table, near, far)


def rounded(values):
    return lax.reduce_precision(values, 8, 7)


def flip(values, name, size, bit):
    return lax.ppermute(values.astype(bf16), name, [(i, i ^ bit) for i in range(size)])


def scattered_axes(dp_axis, experts):
    return ([("dp", dp_axis, 1)] if dp_axis > 1 else []) + [("expert", experts, 1)]


def scatter_table(table, dp_axis, experts):
    for name, size, bit in scattered_axes(dp_axis, experts):
        high = (lax.axis_index(name) & bit) != 0
        rows = table.shape[0] // 2
        low_half, high_half = table[:rows], table[rows:]
        away = jnp.where(high, low_half, high_half)
        table = jnp.where(high, high_half, low_half)
        table = table + flip(away, name, size, bit).astype(f32)
    bit = 2
    while bit < experts:
        table = rounded(table)
        table = table + flip(table, "expert", experts, bit).astype(f32)
        bit *= 2
    return rounded(table).astype(bf16)


def gather_table(table, dp_axis, experts):
    for name, size, bit in reversed(scattered_axes(dp_axis, experts)):
        high = (lax.axis_index(name) & bit) != 0
        other = flip(table, name, size, bit)
        table = jnp.concatenate(
            [jnp.where(high, other, table), jnp.where(high, table, other)], axis=0
        )
    return table.astype(f32)


def local(experts, dp_axis, tokens, cotangent, mixture, stamp, expert_ids, modulation, router, w_gate, w_up, w_down):
    toks, width = tokens.shape
    conditions = modulation.shape[1]
    cap = min(toks, 4 * toks // experts)
    half = experts // 2
    index = lax.axis_index("expert").astype(jnp.int32)
    me = jnp.stack([index, index // half * half, lax.axis_index("dp").astype(jnp.int32)])
    halves = [list(range(half)), list(range(half, experts))]
    across = [(e, (e + half) % experts) for e in range(experts)]

    def hop(array):
        return lax.ppermute(array, "expert", across)

    def trade(array):
        blocks = array.reshape(half, cap, array.shape[1])
        blocks = lax.all_to_all(
            blocks, "expert", split_axis=0, concat_axis=0, tiled=True, axis_index_groups=halves
        )
        return blocks.reshape(array.shape)

    def fan(blocks):
        return [blocks[0]] + [
            lax.ppermute(blocks[k], "expert", [(e, e ^ k) for e in range(experts)])
            for k in range(1, half)
        ]

    def after(array, *others):
        return lax.optimization_barrier((array,) + others)[0]

    meta = jnp.concatenate(
        [expert_ids.T, stamp[None], jnp.zeros((5, toks), jnp.int32)], axis=0
    )
    gate, up, down = (
        lax.all_gather(w[0], "dp", axis=1, tiled=True) for w in (w_gate, w_up, w_down)
    )
    far_tokens = hop(tokens)
    far_meta = hop(meta)
    (near,) = pack(me, after(meta, far_meta), [tokens, cotangent], True, False, half, cap)
    near = trade(near)
    far_cot = hop(after(cotangent, far_tokens))
    far = fan(pack(me, far_meta, [far_tokens], True, True, half, cap))
    far_cots = fan(pack(me, far_meta, [far_cot], False, True, half, cap))

    near_backs, near_late, near_stats = whole(me, [near], modulation, router, down, gate, up)
    near_late, far = lax.optimization_barrier((near_late, far))
    far_in = forward(me, far, modulation, router, gate, up)
    far_backs, far_late, far_stats = backward(
        me, far_cots, modulation, router, *far_in, down, gate, up
    )
    far_back = fan(far_backs)
    lates = [near_late, far_late]
    table = sums(
        me, [[near], far], [near_backs, far_backs], lates, [near_stats, far_stats],
        meta, cotangent, mixture, conditions, experts,
    )
    mine, other = grads(me, lates, *gate.shape)
    merged = merge(me, far_meta, far_back, cap)
    merged, table, other, near_back = lax.optimization_barrier(
        (merged, table, other, near_backs[0])
    )
    far_grad = hop(merged)
    near_back = trade(near_back)
    other = lax.ppermute(other, "dp", [(i, dp_axis - 1 - i) for i in range(dp_axis)])
    table = scatter_table(table, dp_axis, experts)
    d_gate, d_up, d_down = (
        (mine[i].astype(f32) + other[i].astype(f32)).astype(bf16)[None] for i in range(3)
    )
    table, near_back, far_grad, d_gate, d_up, d_down = lax.optimization_barrier(
        (table, near_back, far_grad, d_gate, d_up, d_down)
    )
    table = gather_table(table, dp_axis, experts)
    d_modulation = table[: 3 * conditions].reshape(3, conditions, width)
    d_router = table[3 * conditions : 3 * conditions + experts]
    d_tokens = final(
        me, meta, stamp[:, None], tokens, cotangent, modulation, near_back, far_grad, half, cap
    )
    return (d_tokens, d_gate, d_up, d_down, d_router, d_modulation)


def solution(mesh):
    return jax.shard_map(
        functools.partial(local, mesh.shape["expert"], mesh.shape["dp"]),
        mesh=mesh,
        in_specs=(
            P(("groups", "expert", "dp"), None),
            P(("groups", "expert", "dp"), None),
            P(("groups", "expert", "dp"), None),
            P(("groups", "expert", "dp")),
            P(("groups", "expert", "dp"), None),
            P(),
            P(),
            P("expert", None, "dp"),
            P("expert", None, "dp"),
            P("expert", None, "dp"),
        ),
        out_specs=(
            P(("groups", "expert", "dp"), None),
            P(("groups", "expert"), None, "dp"),
            P(("groups", "expert"), None, "dp"),
            P(("groups", "expert"), None, "dp"),
            P("groups", None),
            P(None, "groups", None),
        ),
        check_vma=False,
    )
```

```python
import functools

import jax
import jax.numpy as jnp
from jax import lax
from jax.experimental import pallas as pl
from jax.experimental.pallas import tpu as pltpu
from jax.sharding import PartitionSpec as P

epsilon = 1e-06
f32 = jnp.float32
bf16 = jnp.bfloat16
LANES = 128
VMEM = pl.BlockSpec(memory_space=pltpu.VMEM)
SMEM = pl.BlockSpec(memory_space=pltpu.SMEM)


def params(mib):
    return pltpu.CompilerParams(vmem_limit_bytes=mib * 1024 * 1024)


def cost(flops, moved):
    return pl.CostEstimate(flops=int(flops), bytes_accessed=int(moved), transcendentals=0)


def dot(a, b, dims=((1,), (0,))):
    return lax.dot_general(a, b, (dims, ((), ())), preferred_element_type=f32)


def routing(base, flip, meta_ref, count, cap):
    toks = meta_ref.shape[1]
    height = max(8, count)
    wanted = base + jnp.bitwise_xor(
        flip, lax.broadcasted_iota(jnp.int32, (height, toks), 0)
    )
    member = jnp.logical_or(meta_ref[0:1, :] == wanted, meta_ref[1:2, :] == wanted)
    earlier = lax.broadcasted_iota(jnp.int32, (toks, toks), 0) < lax.broadcasted_iota(
        jnp.int32, (toks, toks), 1
    )
    slots = dot(member.astype(f32).astype(bf16), earlier.astype(f32).astype(bf16))
    slots = jnp.where(member, slots, -1.0).astype(jnp.int32)
    place = lax.broadcasted_iota(jnp.int32, (cap, toks), 0)
    picks = [(slots[k : k + 1, :] == place).astype(f32) for k in range(count)]
    return jnp.concatenate(picks, axis=0)


def split3(table):
    high = table.astype(bf16)
    rest = table - high.astype(f32)
    middle = rest.astype(bf16)
    low = (rest - middle.astype(f32)).astype(bf16)
    return jnp.concatenate([high, middle, low], axis=0)


def pick3(column, conditions):
    lane = lax.broadcasted_iota(jnp.int32, (column.shape[0], 3 * conditions), 1)
    return (lax.rem(lane, conditions) + 1 == column.astype(jnp.int32)).astype(f32).astype(bf16)


def own_row(me, router_ref):
    table = router_ref[...].astype(f32)
    place = lax.broadcasted_iota(jnp.int32, table.shape, 0)
    return jnp.sum(jnp.where(place == me, table, 0.0), axis=0, keepdims=True)


def normalize(values):
    mean = jnp.mean(values, axis=-1, keepdims=True)
    centred = values - mean
    inverse = lax.rsqrt(jnp.mean(centred * centred, axis=-1, keepdims=True) + epsilon)
    return mean, inverse, centred * inverse


def piece(refs, start, size, columns):
    height = refs[0].shape[0]
    if size <= height:
        block, row = divmod(start, height)
        return refs[block][row : row + size, columns]
    parts = [refs[start // height + i][:, columns] for i in range(size // height)]
    return jnp.concatenate(parts, axis=0)


def put(refs, start, values, columns):
    height = refs[0].shape[0]
    size = values.shape[0]
    if size <= height:
        block, row = divmod(start, height)
        refs[block][row : row + size, columns] = values
    else:
        for i in range(size // height):
            refs[start // height + i][:, columns] = values[i * height : (i + 1) * height]


def pack_kernel(count, cap, number, flipped, stamped, me_ref, meta_ref, *refs):
    arrays, outs = refs[:number], refs[number:]
    flip = me_ref[0] - me_ref[1] if flipped else 0
    picks = routing(me_ref[1], flip, meta_ref, count, cap)
    whole = picks.astype(bf16)
    total = count * cap
    width = arrays[0].shape[1]
    put(outs, 0, dot(whole, arrays[0][...]).astype(bf16), slice(0, width))
    at = width
    if stamped:
        column = jnp.sum(picks * (meta_ref[2:3, :] + 1).astype(f32), axis=1, keepdims=True)
        put(outs, 0, jnp.broadcast_to(column, (total, LANES)).astype(bf16), slice(at, at + LANES))
        at += LANES
    for array in arrays[1:]:
        put(outs, 0, dot(whole, array[...]).astype(bf16), slice(at, at + width))
        at += width


def pack(me, meta, arrays, stamped, flipped, count, cap):
    width = arrays[0].shape[1] * len(arrays) + (LANES if stamped else 0)
    shape = (cap, width) if flipped else (count * cap, width)
    number = count if flipped else 1
    return pl.pallas_call(
        functools.partial(pack_kernel, count, cap, len(arrays), flipped, stamped),
        out_shape=[jax.ShapeDtypeStruct(shape, bf16)] * number,
        in_specs=[SMEM] + [VMEM] * (1 + len(arrays)),
        out_specs=[VMEM] * number,
        compiler_params=params(8),
        cost_estimate=cost(1e9, 4e6),
        name="pack",
    )(me, meta, *arrays)


def late_views(late_ref, width, full):
    edges = [0, width, 2 * width, 2 * width + full, 2 * width + 2 * full, 2 * width + 3 * full]
    return [late_ref.at[:, low:high] for low, high in zip(edges, edges[1:])]


def forward_body(me_ref, ins, table_ref, router_ref, gate_ref, up_ref, mod_ref, stats_ref, act_ref, fac_ref, hid_ref):
    count, width = mod_ref.shape
    full = gate_ref.shape[1]
    conditions = table_ref.shape[1]
    chunk = 64
    shift_parts, scale_parts = split3(table_ref[0]), split3(table_ref[1])
    router_row = own_row(me_ref[0], router_ref)
    lane = lax.broadcasted_iota(jnp.int32, (chunk, LANES), 1)
    for start in range(0, count, chunk):
        part = slice(start, start + chunk)
        mean, inverse, normed = normalize(piece(ins, start, chunk, slice(0, width)).astype(f32))
        mark = piece(ins, start, chunk, slice(width, width + 1)).astype(f32)
        pick = pick3(mark, conditions)
        rows = (normed * (1.0 + dot(pick, scale_parts)) + dot(pick, shift_parts)).astype(bf16)
        mod_ref[part, :] = rows
        logit = jnp.sum(rows.astype(f32) * router_row, axis=1, keepdims=True)
        prob = jax.nn.sigmoid(logit)
        stats_ref[part, :] = jnp.where(
            lane == 0, mean, jnp.where(lane == 1, inverse, jnp.where(lane == 2, prob, mark))
        )
    step = 256
    for start in range(0, full, step):
        columns = slice(start, start + step)
        pre_gate = dot(mod_ref[...], gate_ref[:, columns])
        pre_up = dot(mod_ref[...], up_ref[:, columns])
        sig = jax.nn.sigmoid(pre_gate)
        active = pre_gate * sig
        act_ref[:, columns] = active
        fac_ref[:, columns] = pre_up * sig * (1.0 + pre_gate * (1.0 - sig))
        hid_ref[:, columns] = (active * pre_up).astype(bf16)


def backward_body(offset, me_ref, cots, table_ref, router_ref, stats_ref, act_ref, fac_ref, hid_ref, down_ref, gate_ref, up_ref, backs, og_ref, gg_ref, ug_ref, lg_ref, ups_ref):
    count, width = og_ref.shape
    full = gate_ref.shape[1]
    conditions = table_ref.shape[1]
    gate_parts = split3(table_ref[2])
    prob = stats_ref[:, 2:3]
    chunk = 64
    for start in range(0, count, chunk):
        part = slice(start, start + chunk)
        pick = pick3(stats_ref[part, 3:4], conditions)
        cot = piece(cots, start, chunk, slice(offset, offset + width)).astype(f32)
        upstream = (dot(pick, gate_parts) * cot).astype(bf16)
        ups_ref[part, :] = upstream
        og_ref[part, :] = (stats_ref[part, 2:3] * upstream.astype(f32)).astype(bf16)
    prob_grad = jnp.zeros((count, 1), f32)
    step = 256
    for start in range(0, full, step):
        columns = slice(start, start + step)
        raw = dot(ups_ref[...], down_ref[:, columns])
        prob_grad += jnp.sum(hid_ref[:, columns].astype(f32) * raw, axis=1, keepdims=True)
        hidden_grad = prob * raw
        gg_ref[:, columns] = (hidden_grad * fac_ref[:, columns]).astype(bf16)
        ug_ref[:, columns] = (hidden_grad * act_ref[:, columns]).astype(bf16)
    logit_grad = prob_grad * prob * (1.0 - prob)
    lane = lax.broadcasted_iota(jnp.int32, stats_ref.shape, 1)
    lg_ref[...] = jnp.where(lane == 4, logit_grad, stats_ref[...])
    router_row = own_row(me_ref[0], router_ref)
    for start in range(0, width, step):
        part = slice(start, start + step)
        total = dot(gg_ref[...], gate_ref[part, :], ((1,), (1,)))
        total += dot(ug_ref[...], up_ref[part, :], ((1,), (1,)))
        put(backs, 0, (total + logit_grad * router_row[:, part]).astype(bf16), part)


def forward_kernel(number, me_ref, *refs):
    forward_body(me_ref, refs[:number], *refs[number:])


def forward(me, blocks, table, router, gate, up):
    count = sum(block.shape[0] for block in blocks)
    width, full = gate.shape
    wide = jax.ShapeDtypeStruct((count, full), f32)
    return pl.pallas_call(
        functools.partial(forward_kernel, len(blocks)),
        out_shape=[
            jax.ShapeDtypeStruct((count, width), bf16),
            jax.ShapeDtypeStruct((count, LANES), f32),
            wide,
            wide,
            jax.ShapeDtypeStruct((count, full), bf16),
        ],
        in_specs=[SMEM] + [VMEM] * (len(blocks) + 4),
        out_specs=[VMEM] * 5,
        compiler_params=params(12),
        cost_estimate=cost(4 * count * width * full, 4 * width * full + count * 12000),
        name="expert_in",
    )(me, *blocks, table, router, gate, up)


def backward_shapes(blocks, width, full):
    count = sum(block.shape[0] for block in blocks)
    return [jax.ShapeDtypeStruct((block.shape[0], width), bf16) for block in blocks] + [
        jax.ShapeDtypeStruct((count, 2 * width + 3 * full), bf16),
        jax.ShapeDtypeStruct((count, LANES), f32),
    ]


def backward_kernel(number, me_ref, *refs):
    cots, refs = refs[:number], refs[number:]
    table_ref, router_ref, seen_ref, stats_ref, act_ref, fac_ref, hid_ref, down_ref, gate_ref, up_ref = refs[:10]
    backs, (late_ref, lg_ref, ups_ref) = refs[10 : 10 + number], refs[10 + number :]
    mod, og, gg, ug, hid = late_views(late_ref, *gate_ref.shape)
    backward_body(0, me_ref, cots, table_ref, router_ref, stats_ref, act_ref, fac_ref, hid_ref, down_ref, gate_ref, up_ref, backs, og, gg, ug, lg_ref, ups_ref)
    mod[...] = seen_ref[...]
    hid[...] = hid_ref[...]


def backward(me, blocks, table, router, mod, stats, act, fac, hid, down, gate, up):
    count = sum(block.shape[0] for block in blocks)
    width, full = gate.shape
    number = len(blocks)
    outs = pl.pallas_call(
        functools.partial(backward_kernel, number),
        out_shape=backward_shapes(blocks, width, full),
        in_specs=[SMEM] + [VMEM] * (number + 10),
        out_specs=[VMEM] * (number + 2),
        scratch_shapes=[pltpu.VMEM((count, width), bf16)],
        compiler_params=params(12),
        cost_estimate=cost(6 * count * width * full, 6 * width * full + count * 16000),
        name="expert_back",
    )(me, *blocks, table, router, mod, stats, act, fac, hid, down, gate, up)
    return outs[:number], *outs[number:]


def whole_kernel(number, me_ref, *refs):
    blocks, refs = refs[:number], refs[number:]
    table_ref, router_ref, down_ref, gate_ref, up_ref = refs[:5]
    backs, refs = refs[5 : 5 + number], refs[5 + number :]
    late_ref, lg_ref, stats_ref, act_ref, fac_ref, ups_ref = refs
    mod, og, gg, ug, hid = late_views(late_ref, *gate_ref.shape)
    forward_body(me_ref, blocks, table_ref, router_ref, gate_ref, up_ref, mod, stats_ref, act_ref, fac_ref, hid)
    backward_body(mod.shape[1] + LANES, me_ref, blocks, table_ref, router_ref, stats_ref, act_ref, fac_ref, hid, down_ref, gate_ref, up_ref, backs, og, gg, ug, lg_ref, ups_ref)


def whole(me, blocks, table, router, down, gate, up):
    count = sum(block.shape[0] for block in blocks)
    width, full = gate.shape
    number = len(blocks)
    outs = pl.pallas_call(
        functools.partial(whole_kernel, number),
        out_shape=backward_shapes(blocks, width, full),
        in_specs=[SMEM] + [VMEM] * (number + 5),
        out_specs=[VMEM] * (number + 2),
        scratch_shapes=[pltpu.VMEM((count, LANES), f32)]
        + [pltpu.VMEM((count, full), f32)] * 2
        + [pltpu.VMEM((count, width), bf16)],
        compiler_params=params(16),
        cost_estimate=cost(10 * count * width * full, 6 * width * full + count * 16000),
        name="expert_whole",
    )(me, *blocks, table, router, down, gate, up)
    return outs[:number], *outs[number:]


def sums_kernel(numbers, tall, me_ref, *refs):
    rows, backs = [], []
    for group in (rows, backs):
        for number in numbers:
            group.append(refs[:number])
            refs = refs[number:]
    lates, stats = refs[:2], refs[2:4]
    meta_ref, cot_ref, mix_ref, out_ref = refs[4:]
    count, width = lates[0].shape[0], cot_ref.shape[1]
    conditions, experts = tall
    zero = ((0,), (0,))
    shift_sum = jnp.zeros((conditions, width), f32)
    scale_sum = jnp.zeros((conditions, width), f32)
    router_sum = jnp.zeros((1, width), f32)
    chunk = 128
    for q in range(2):
        for start in range(0, count, chunk):
            part = slice(start, start + chunk)
            lane = lax.broadcasted_iota(jnp.int32, (chunk, conditions), 1)
            mark = stats[q][part, 3:4].astype(jnp.int32)
            pick = (lane + 1 == mark).astype(f32).astype(bf16)
            back = piece(backs[q], start, chunk, slice(0, width))
            mean, inverse = stats[q][part, 0:1], stats[q][part, 1:2]
            values = piece(rows[q], start, chunk, slice(0, width)).astype(f32)
            normed = (values - mean) * inverse
            product = back.astype(f32) * normed
            high = product.astype(bf16)
            low = (product - high.astype(f32)).astype(bf16)
            shift_sum += dot(pick, back, zero)
            scale_sum += dot(pick, high, zero) + dot(pick, low, zero)
            weighted = stats[q][part, 4:5] * lates[q][part, :width].astype(f32)
            router_sum += jnp.sum(weighted, axis=0, keepdims=True)
    toks = cot_ref.shape[0]
    wanted = lax.broadcasted_iota(jnp.int32, (conditions, toks), 0)
    pick = (meta_ref[2:3, :] == wanted).astype(f32).astype(bf16)
    product = cot_ref[...].astype(f32) * mix_ref[...].astype(f32)
    high = product.astype(bf16)
    low = (product - high.astype(f32)).astype(bf16)
    out_ref[0:conditions, :] = shift_sum
    out_ref[conditions : 2 * conditions, :] = scale_sum
    out_ref[2 * conditions : 3 * conditions, :] = dot(pick, high) + dot(pick, low)
    place = lax.broadcasted_iota(jnp.int32, (out_ref.shape[0] - 3 * conditions, width), 0)
    out_ref[3 * conditions :, :] = jnp.where(place == me_ref[0], router_sum, 0.0)


def sums(me, rows, backs, lates, stats, meta, cot, mix, conditions, experts):
    numbers = [len(blocks) for blocks in rows]
    height = -(-(3 * conditions + experts) // 128) * 128
    width = cot.shape[1]
    return pl.pallas_call(
        functools.partial(sums_kernel, numbers, (conditions, experts)),
        out_shape=jax.ShapeDtypeStruct((height, width), f32),
        in_specs=[SMEM] + [VMEM] * (2 * sum(numbers) + 7),
        out_specs=VMEM,
        compiler_params=params(12),
        cost_estimate=cost(1e6, 1e4),
        name="table_sums",
    )(me, *rows[0], *rows[1], *backs[0], *backs[1], *lates, *stats, meta, cot, mix)


def grads_kernel(me_ref, near_ref, far_ref, *outs):
    width, half = outs[0].shape
    other_ref = outs[3]
    zero = ((0,), (0,))
    second = me_ref[2] != 0
    step = 256
    near, far = (late_views(ref, width, 2 * half) for ref in (near_ref, far_ref))
    for start in range(0, width, step):
        part = slice(start, start + step)
        for index, (left, right) in enumerate(((0, 2), (0, 3), (1, 4))):
            total = dot(near[left][:, part], near[right][...], zero)
            total += dot(far[left][:, part], far[right][...], zero)
            low, high = total[:, :half], total[:, half:]
            outs[index][part, :] = jnp.where(second, high, low).astype(bf16)
            other_ref[index, part, :] = jnp.where(second, low, high).astype(bf16)


def grads(me, lates, width, full):
    outs = pl.pallas_call(
        grads_kernel,
        out_shape=[jax.ShapeDtypeStruct((width, full // 2), bf16)] * 3
        + [jax.ShapeDtypeStruct((3, width, full // 2), bf16)],
        in_specs=[SMEM] + [VMEM] * 2,
        out_specs=[VMEM] * 4,
        compiler_params=params(12),
        cost_estimate=cost(1e6, 1e4),
        name="weight_grads",
    )(me, *lates)
    return outs[:3], outs[3]


def merge_kernel(count, cap, me_ref, meta_ref, *refs):
    picks = routing(me_ref[1], me_ref[0] - me_ref[1], meta_ref, count, cap).astype(bf16)
    rows = piece(refs[:-1], 0, count * cap, slice(None))
    refs[-1][...] = dot(picks, rows, ((0,), (0,))).astype(bf16)


def merge(me, meta, backs, cap):
    return pl.pallas_call(
        functools.partial(merge_kernel, len(backs), cap),
        out_shape=jax.ShapeDtypeStruct((meta.shape[1], backs[0].shape[1]), bf16),
        in_specs=[SMEM] + [VMEM] * (1 + len(backs)),
        out_specs=VMEM,
        compiler_params=params(8),
        cost_estimate=cost(1e9, 2e6),
        name="merge",
    )(me, meta, *backs)


def final_kernel(count, cap, me_ref, meta_ref, stamp_ref, tok_ref, cot_ref, table_ref, near_ref, far_ref, out_ref):
    picks = routing(me_ref[1], 0, meta_ref, count, cap).astype(bf16)
    mod_grad = dot(picks, near_ref[...], ((0,), (0,))) + far_ref[...].astype(f32)
    conditions = table_ref.shape[1]
    _, inverse, normed = normalize(tok_ref[...].astype(f32))
    pick = pick3((stamp_ref[:, 0:1] + 1).astype(f32), conditions)
    d_normed = mod_grad * (1.0 + dot(pick, split3(table_ref[1])))
    d_input = inverse * (
        d_normed
        - jnp.mean(d_normed, axis=-1, keepdims=True)
        - normed * jnp.mean(d_normed * normed, axis=-1, keepdims=True)
    )
    out_ref[...] = (cot_ref[...].astype(f32) + d_input).astype(bf16)


def final(me, meta, stamp_column, tokens, cot, table, near, far, count, cap):
    return pl.pallas_call(
        functools.partial(final_kernel, count, cap),
        out_shape=jax.ShapeDtypeStruct(tokens.shape, bf16),
        in_specs=[SMEM] + [VMEM] * 7,
        out_specs=VMEM,
        compiler_params=params(12),
        cost_estimate=cost(1e9, 4e6),
        name="final",
    )(me, meta, stamp_column, tokens, cot, table, near, far)


def rounded(values):
    return lax.reduce_precision(values, 8, 7)


def flip(values, name, size, bit):
    return lax.ppermute(values.astype(bf16), name, [(i, i ^ bit) for i in range(size)])


def scattered_axes(dp_axis, experts):
    return ([("dp", dp_axis, 1)] if dp_axis > 1 else []) + [("expert", experts, 1)]


def scatter_table(table, dp_axis, experts):
    for name, size, bit in scattered_axes(dp_axis, experts):
        high = (lax.axis_index(name) & bit) != 0
        rows = table.shape[0] // 2
        low_half, high_half = table[:rows], table[rows:]
        away = jnp.where(high, low_half, high_half)
        table = jnp.where(high, high_half, low_half)
        table = table + flip(away, name, size, bit).astype(f32)
    return table


def exchange_table(table, experts, first, last):
    bit = first
    while bit < last:
        table = rounded(table)
        table = table + flip(table, "expert", experts, bit).astype(f32)
        bit *= 2
    return table


def add_kernel(other_ref, *refs):
    number = len(refs) // 2
    for i in range(number):
        total = refs[i][...].astype(f32) + other_ref[i].astype(f32)
        refs[number + i][0] = total.astype(bf16)


def add(mine, other):
    width, half = mine[0].shape
    step = 256
    part = pl.BlockSpec((step, half), lambda i: (i, 0))
    return pl.pallas_call(
        add_kernel,
        grid=(width // step,),
        out_shape=[jax.ShapeDtypeStruct((1, width, half), bf16)] * len(mine),
        in_specs=[pl.BlockSpec((len(mine), step, half), lambda i: (0, i, 0))] + [part] * len(mine),
        out_specs=[pl.BlockSpec((1, step, half), lambda i: (0, i, 0))] * len(mine),
        compiler_params=params(12),
        cost_estimate=cost(1e6, 1e4),
        name="add",
    )(other, *mine)


def gather_table(table, dp_axis, experts):
    for name, size, bit in reversed(scattered_axes(dp_axis, experts)):
        high = (lax.axis_index(name) & bit) != 0
        other = flip(table, name, size, bit)
        table = jnp.concatenate(
            [jnp.where(high, other, table), jnp.where(high, table, other)], axis=0
        )
    return table


def local(experts, dp_axis, tokens, cotangent, mixture, stamp, expert_ids, modulation, router, w_gate, w_up, w_down):
    toks, width = tokens.shape
    conditions = modulation.shape[1]
    cap = min(toks, 4 * toks // experts)
    half = experts // 2
    index = lax.axis_index("expert").astype(jnp.int32)
    me = jnp.stack([index, index // half * half, lax.axis_index("dp").astype(jnp.int32)])
    halves = [list(range(half)), list(range(half, experts))]
    across = [(e, (e + half) % experts) for e in range(experts)]

    def hop(array):
        return lax.ppermute(array, "expert", across)

    def trade(array):
        blocks = array.reshape(half, cap, array.shape[1])
        blocks = lax.all_to_all(
            blocks, "expert", split_axis=0, concat_axis=0, tiled=True, axis_index_groups=halves
        )
        return blocks.reshape(array.shape)

    def fan(blocks):
        return [blocks[0]] + [
            lax.ppermute(blocks[k], "expert", [(e, e ^ k) for e in range(experts)])
            for k in range(1, half)
        ]

    def after(array, *others):
        return lax.optimization_barrier((array,) + others)[0]

    meta = jnp.concatenate(
        [expert_ids.T, stamp[None], jnp.zeros((5, toks), jnp.int32)], axis=0
    )
    gate, up, down = (
        lax.all_gather(w[0], "dp", axis=1, tiled=True) for w in (w_gate, w_up, w_down)
    )
    far_tokens = hop(tokens)
    far_meta = hop(meta)
    (near,) = pack(me, meta, [tokens, cotangent], True, False, half, cap)
    far_tokens, near, far_meta = lax.optimization_barrier((far_tokens, near, far_meta))
    near = trade(near)
    far_cot = hop(after(cotangent, far_tokens))
    far = fan(pack(me, far_meta, [far_tokens], True, True, half, cap))
    far_cots = fan(pack(me, far_meta, [far_cot], False, True, half, cap))

    near_backs, near_late, near_stats = whole(me, [near], modulation, router, down, gate, up)
    near_late, far = lax.optimization_barrier((near_late, far))
    far_in = forward(me, far, modulation, router, gate, up)
    far_backs, far_late, far_stats = backward(
        me, far_cots, modulation, router, *far_in, down, gate, up
    )
    far_back = fan(far_backs)
    lates = [near_late, far_late]
    table = sums(
        me, [[near], far], [near_backs, far_backs], lates, [near_stats, far_stats],
        meta, cotangent, mixture, conditions, experts,
    )
    mine, other = grads(me, lates, *gate.shape)
    merged = merge(me, far_meta, far_back, cap)
    merged, table, other, near_back = lax.optimization_barrier(
        (merged, table, other, near_backs[0])
    )
    far_grad = hop(merged)
    near_back = trade(near_back)
    other = lax.ppermute(other, "dp", [(i, dp_axis - 1 - i) for i in range(dp_axis)])
    table = scatter_table(table, dp_axis, experts)
    table = exchange_table(table, experts, 2, 2)
    d_gate, d_up, d_down = add(mine, other)
    table, near_back, far_grad, d_gate, d_up, d_down = lax.optimization_barrier(
        (table, near_back, far_grad, d_gate, d_up, d_down)
    )
    table = rounded(exchange_table(table, experts, 2, experts)).astype(bf16)
    table = gather_table(table, dp_axis, experts)
    d_tokens = final(
        me, meta, stamp[:, None], tokens, cotangent, modulation, near_back, far_grad, half, cap
    )
    table, d_tokens = lax.optimization_barrier((table, d_tokens))
    table = table.astype(f32)
    d_modulation = table[: 3 * conditions].reshape(3, conditions, width)
    d_router = table[3 * conditions : 3 * conditions + experts]
    return (d_tokens, d_gate, d_up, d_down, d_router, d_modulation)


def solution(mesh):
    return jax.shard_map(
        functools.partial(local, mesh.shape["expert"], mesh.shape["dp"]),
        mesh=mesh,
        in_specs=(
            P(("groups", "expert", "dp"), None),
            P(("groups", "expert", "dp"), None),
            P(("groups", "expert", "dp"), None),
            P(("groups", "expert", "dp")),
            P(("groups", "expert", "dp"), None),
            P(),
            P(),
            P("expert", None, "dp"),
            P("expert", None, "dp"),
            P("expert", None, "dp"),
        ),
        out_specs=(
            P(("groups", "expert", "dp"), None),
            P(("groups", "expert"), None, "dp"),
            P(("groups", "expert"), None, "dp"),
            P(("groups", "expert"), None, "dp"),
            P("groups", None),
            P(None, "groups", None),
        ),
        check_vma=False,
    )
```

```python
import functools

import jax
import jax.numpy as jnp
from jax import lax
from jax.experimental import pallas as pl
from jax.experimental.pallas import tpu as pltpu
from jax.sharding import PartitionSpec as P

epsilon = 1e-06
f32 = jnp.float32
bf16 = jnp.bfloat16
LANES = 128
VMEM = pl.BlockSpec(memory_space=pltpu.VMEM)
SMEM = pl.BlockSpec(memory_space=pltpu.SMEM)


def params(mib):
    return pltpu.CompilerParams(vmem_limit_bytes=mib * 1024 * 1024)


def cost(flops, moved):
    return pl.CostEstimate(flops=int(flops), bytes_accessed=int(moved), transcendentals=0)


def dot(a, b, dims=((1,), (0,))):
    return lax.dot_general(a, b, (dims, ((), ())), preferred_element_type=f32)


def routing(base, flip, meta_ref, count, cap):
    toks = meta_ref.shape[1]
    height = max(8, count)
    wanted = base + jnp.bitwise_xor(
        flip, lax.broadcasted_iota(jnp.int32, (height, toks), 0)
    )
    member = jnp.logical_or(meta_ref[0:1, :] == wanted, meta_ref[1:2, :] == wanted)
    earlier = lax.broadcasted_iota(jnp.int32, (toks, toks), 0) < lax.broadcasted_iota(
        jnp.int32, (toks, toks), 1
    )
    slots = dot(member.astype(f32).astype(bf16), earlier.astype(f32).astype(bf16))
    slots = jnp.where(member, slots, -1.0).astype(jnp.int32)
    place = lax.broadcasted_iota(jnp.int32, (cap, toks), 0)
    picks = [(slots[k : k + 1, :] == place).astype(f32) for k in range(count)]
    return jnp.concatenate(picks, axis=0)


def split3(table):
    high = table.astype(bf16)
    rest = table - high.astype(f32)
    middle = rest.astype(bf16)
    low = (rest - middle.astype(f32)).astype(bf16)
    return jnp.concatenate([high, middle, low], axis=0)


def pick3(column, conditions):
    lane = lax.broadcasted_iota(jnp.int32, (column.shape[0], 3 * conditions), 1)
    return (lax.rem(lane, conditions) + 1 == column.astype(jnp.int32)).astype(f32).astype(bf16)


def own_row(me, router_ref):
    table = router_ref[...].astype(f32)
    place = lax.broadcasted_iota(jnp.int32, table.shape, 0)
    return jnp.sum(jnp.where(place == me, table, 0.0), axis=0, keepdims=True)


def normalize(values):
    mean = jnp.mean(values, axis=-1, keepdims=True)
    centred = values - mean
    inverse = lax.rsqrt(jnp.mean(centred * centred, axis=-1, keepdims=True) + epsilon)
    return mean, inverse, centred * inverse


def piece(refs, start, size, columns):
    height = refs[0].shape[0]
    if size <= height:
        block, row = divmod(start, height)
        return refs[block][row : row + size, columns]
    parts = [refs[start // height + i][:, columns] for i in range(size // height)]
    return jnp.concatenate(parts, axis=0)


def put(refs, start, values, columns):
    height = refs[0].shape[0]
    size = values.shape[0]
    if size <= height:
        block, row = divmod(start, height)
        refs[block][row : row + size, columns] = values
    else:
        for i in range(size // height):
            refs[start // height + i][:, columns] = values[i * height : (i + 1) * height]


def pack_kernel(count, cap, number, flipped, stamped, me_ref, meta_ref, *refs):
    arrays, outs = refs[:number], refs[number:]
    flip = me_ref[0] - me_ref[1] if flipped else 0
    picks = routing(me_ref[1], flip, meta_ref, count, cap)
    whole = picks.astype(bf16)
    total = count * cap
    width = arrays[0].shape[1]
    put(outs, 0, dot(whole, arrays[0][...]).astype(bf16), slice(0, width))
    at = width
    if stamped:
        column = jnp.sum(picks * (meta_ref[2:3, :] + 1).astype(f32), axis=1, keepdims=True)
        put(outs, 0, jnp.broadcast_to(column, (total, LANES)).astype(bf16), slice(at, at + LANES))
        at += LANES
    for array in arrays[1:]:
        put(outs, 0, dot(whole, array[...]).astype(bf16), slice(at, at + width))
        at += width


def pack(me, meta, arrays, stamped, flipped, count, cap):
    width = arrays[0].shape[1] * len(arrays) + (LANES if stamped else 0)
    shape = (cap, width) if flipped else (count * cap, width)
    number = count if flipped else 1
    return pl.pallas_call(
        functools.partial(pack_kernel, count, cap, len(arrays), flipped, stamped),
        out_shape=[jax.ShapeDtypeStruct(shape, bf16)] * number,
        in_specs=[SMEM] + [VMEM] * (1 + len(arrays)),
        out_specs=[VMEM] * number,
        compiler_params=params(8),
        cost_estimate=cost(1e9, 4e6),
        name="pack",
    )(me, meta, *arrays)


def late_views(late_ref, width, full):
    edges = [0, width, 2 * width, 2 * width + full, 2 * width + 2 * full, 2 * width + 3 * full]
    return [late_ref.at[:, low:high] for low, high in zip(edges, edges[1:])]


def forward_body(me_ref, ins, table_ref, router_ref, gate_ref, up_ref, mod_ref, stats_ref, act_ref, fac_ref, hid_ref):
    count, width = mod_ref.shape
    full = gate_ref.shape[1]
    conditions = table_ref.shape[1]
    chunk = 64
    shift_parts, scale_parts = split3(table_ref[0]), split3(table_ref[1])
    router_row = own_row(me_ref[0], router_ref)
    lane = lax.broadcasted_iota(jnp.int32, (chunk, LANES), 1)
    for start in range(0, count, chunk):
        part = slice(start, start + chunk)
        mean, inverse, normed = normalize(piece(ins, start, chunk, slice(0, width)).astype(f32))
        mark = piece(ins, start, chunk, slice(width, width + 1)).astype(f32)
        pick = pick3(mark, conditions)
        rows = (normed * (1.0 + dot(pick, scale_parts)) + dot(pick, shift_parts)).astype(bf16)
        mod_ref[part, :] = rows
        logit = jnp.sum(rows.astype(f32) * router_row, axis=1, keepdims=True)
        prob = jax.nn.sigmoid(logit)
        stats_ref[part, :] = jnp.where(
            lane == 0, mean, jnp.where(lane == 1, inverse, jnp.where(lane == 2, prob, mark))
        )
    step = 256
    for start in range(0, full, step):
        columns = slice(start, start + step)
        pre_gate = dot(mod_ref[...], gate_ref[:, columns])
        pre_up = dot(mod_ref[...], up_ref[:, columns])
        sig = jax.nn.sigmoid(pre_gate)
        active = pre_gate * sig
        act_ref[:, columns] = active
        fac_ref[:, columns] = pre_up * sig * (1.0 + pre_gate * (1.0 - sig))
        hid_ref[:, columns] = (active * pre_up).astype(bf16)


def backward_body(offset, me_ref, cots, table_ref, router_ref, stats_ref, act_ref, fac_ref, hid_ref, down_ref, gate_ref, up_ref, backs, og_ref, gg_ref, ug_ref, lg_ref, ups_ref):
    count, width = og_ref.shape
    full = gate_ref.shape[1]
    conditions = table_ref.shape[1]
    gate_parts = split3(table_ref[2])
    prob = stats_ref[:, 2:3]
    chunk = 64
    for start in range(0, count, chunk):
        part = slice(start, start + chunk)
        pick = pick3(stats_ref[part, 3:4], conditions)
        cot = piece(cots, start, chunk, slice(offset, offset + width)).astype(f32)
        upstream = (dot(pick, gate_parts) * cot).astype(bf16)
        ups_ref[part, :] = upstream
        og_ref[part, :] = (stats_ref[part, 2:3] * upstream.astype(f32)).astype(bf16)
    prob_grad = jnp.zeros((count, 1), f32)
    step = 256
    for start in range(0, full, step):
        columns = slice(start, start + step)
        raw = dot(ups_ref[...], down_ref[:, columns])
        prob_grad += jnp.sum(hid_ref[:, columns].astype(f32) * raw, axis=1, keepdims=True)
        hidden_grad = prob * raw
        gg_ref[:, columns] = (hidden_grad * fac_ref[:, columns]).astype(bf16)
        ug_ref[:, columns] = (hidden_grad * act_ref[:, columns]).astype(bf16)
    logit_grad = prob_grad * prob * (1.0 - prob)
    lane = lax.broadcasted_iota(jnp.int32, stats_ref.shape, 1)
    lg_ref[...] = jnp.where(lane == 4, logit_grad, stats_ref[...])
    router_row = own_row(me_ref[0], router_ref)
    for start in range(0, width, step):
        part = slice(start, start + step)
        total = dot(gg_ref[...], gate_ref[part, :], ((1,), (1,)))
        total += dot(ug_ref[...], up_ref[part, :], ((1,), (1,)))
        put(backs, 0, (total + logit_grad * router_row[:, part]).astype(bf16), part)


def forward_kernel(number, me_ref, *refs):
    forward_body(me_ref, refs[:number], *refs[number:])


def forward(me, blocks, table, router, gate, up):
    count = sum(block.shape[0] for block in blocks)
    width, full = gate.shape
    wide = jax.ShapeDtypeStruct((count, full), f32)
    return pl.pallas_call(
        functools.partial(forward_kernel, len(blocks)),
        out_shape=[
            jax.ShapeDtypeStruct((count, width), bf16),
            jax.ShapeDtypeStruct((count, LANES), f32),
            wide,
            wide,
            jax.ShapeDtypeStruct((count, full), bf16),
        ],
        in_specs=[SMEM] + [VMEM] * (len(blocks) + 4),
        out_specs=[VMEM] * 5,
        compiler_params=params(12),
        cost_estimate=cost(4 * count * width * full, 4 * width * full + count * 12000),
        name="expert_in",
    )(me, *blocks, table, router, gate, up)


def backward_shapes(blocks, width, full):
    count = sum(block.shape[0] for block in blocks)
    return [jax.ShapeDtypeStruct((block.shape[0], width), bf16) for block in blocks] + [
        jax.ShapeDtypeStruct((count, 2 * width + 3 * full), bf16),
        jax.ShapeDtypeStruct((count, LANES), f32),
    ]


def backward_kernel(number, me_ref, *refs):
    cots, refs = refs[:number], refs[number:]
    table_ref, router_ref, seen_ref, stats_ref, act_ref, fac_ref, hid_ref, down_ref, gate_ref, up_ref = refs[:10]
    backs, (late_ref, lg_ref, ups_ref) = refs[10 : 10 + number], refs[10 + number :]
    mod, og, gg, ug, hid = late_views(late_ref, *gate_ref.shape)
    backward_body(0, me_ref, cots, table_ref, router_ref, stats_ref, act_ref, fac_ref, hid_ref, down_ref, gate_ref, up_ref, backs, og, gg, ug, lg_ref, ups_ref)
    mod[...] = seen_ref[...]
    hid[...] = hid_ref[...]


def backward(me, blocks, table, router, mod, stats, act, fac, hid, down, gate, up):
    count = sum(block.shape[0] for block in blocks)
    width, full = gate.shape
    number = len(blocks)
    outs = pl.pallas_call(
        functools.partial(backward_kernel, number),
        out_shape=backward_shapes(blocks, width, full),
        in_specs=[SMEM] + [VMEM] * (number + 10),
        out_specs=[VMEM] * (number + 2),
        scratch_shapes=[pltpu.VMEM((count, width), bf16)],
        compiler_params=params(12),
        cost_estimate=cost(6 * count * width * full, 6 * width * full + count * 16000),
        name="expert_back",
    )(me, *blocks, table, router, mod, stats, act, fac, hid, down, gate, up)
    return outs[:number], *outs[number:]


def whole_kernel(number, me_ref, *refs):
    blocks, refs = refs[:number], refs[number:]
    table_ref, router_ref, down_ref, gate_ref, up_ref = refs[:5]
    backs, refs = refs[5 : 5 + number], refs[5 + number :]
    late_ref, lg_ref, stats_ref, act_ref, fac_ref, ups_ref = refs
    mod, og, gg, ug, hid = late_views(late_ref, *gate_ref.shape)
    forward_body(me_ref, blocks, table_ref, router_ref, gate_ref, up_ref, mod, stats_ref, act_ref, fac_ref, hid)
    backward_body(mod.shape[1] + LANES, me_ref, blocks, table_ref, router_ref, stats_ref, act_ref, fac_ref, hid, down_ref, gate_ref, up_ref, backs, og, gg, ug, lg_ref, ups_ref)


def whole(me, blocks, table, router, down, gate, up):
    count = sum(block.shape[0] for block in blocks)
    width, full = gate.shape
    number = len(blocks)
    outs = pl.pallas_call(
        functools.partial(whole_kernel, number),
        out_shape=backward_shapes(blocks, width, full),
        in_specs=[SMEM] + [VMEM] * (number + 5),
        out_specs=[VMEM] * (number + 2),
        scratch_shapes=[pltpu.VMEM((count, LANES), f32)]
        + [pltpu.VMEM((count, full), f32)] * 2
        + [pltpu.VMEM((count, width), bf16)],
        compiler_params=params(16),
        cost_estimate=cost(10 * count * width * full, 6 * width * full + count * 16000),
        name="expert_whole",
    )(me, *blocks, table, router, down, gate, up)
    return outs[:number], *outs[number:]


def sums_kernel(numbers, tall, me_ref, *refs):
    rows, backs = [], []
    for group in (rows, backs):
        for number in numbers:
            group.append(refs[:number])
            refs = refs[number:]
    lates, stats = refs[:2], refs[2:4]
    meta_ref, cot_ref, mix_ref, out_ref = refs[4:]
    count, width = lates[0].shape[0], cot_ref.shape[1]
    conditions, experts = tall
    zero = ((0,), (0,))
    shift_sum = jnp.zeros((conditions, width), f32)
    scale_sum = jnp.zeros((conditions, width), f32)
    router_sum = jnp.zeros((1, width), f32)
    chunk = 128
    for q in range(2):
        for start in range(0, count, chunk):
            part = slice(start, start + chunk)
            lane = lax.broadcasted_iota(jnp.int32, (chunk, conditions), 1)
            mark = stats[q][part, 3:4].astype(jnp.int32)
            pick = (lane + 1 == mark).astype(f32).astype(bf16)
            back = piece(backs[q], start, chunk, slice(0, width))
            mean, inverse = stats[q][part, 0:1], stats[q][part, 1:2]
            values = piece(rows[q], start, chunk, slice(0, width)).astype(f32)
            normed = (values - mean) * inverse
            product = back.astype(f32) * normed
            high = product.astype(bf16)
            low = (product - high.astype(f32)).astype(bf16)
            shift_sum += dot(pick, back, zero)
            scale_sum += dot(pick, high, zero) + dot(pick, low, zero)
            weighted = stats[q][part, 4:5] * lates[q][part, :width].astype(f32)
            router_sum += jnp.sum(weighted, axis=0, keepdims=True)
    toks = cot_ref.shape[0]
    wanted = lax.broadcasted_iota(jnp.int32, (conditions, toks), 0)
    pick = (meta_ref[2:3, :] == wanted).astype(f32).astype(bf16)
    product = cot_ref[...].astype(f32) * mix_ref[...].astype(f32)
    high = product.astype(bf16)
    low = (product - high.astype(f32)).astype(bf16)
    out_ref[0:conditions, :] = shift_sum
    out_ref[conditions : 2 * conditions, :] = scale_sum
    out_ref[2 * conditions : 3 * conditions, :] = dot(pick, high) + dot(pick, low)
    place = lax.broadcasted_iota(jnp.int32, (out_ref.shape[0] - 3 * conditions, width), 0)
    out_ref[3 * conditions :, :] = jnp.where(place == me_ref[0], router_sum, 0.0)


def sums(me, rows, backs, lates, stats, meta, cot, mix, conditions, experts):
    numbers = [len(blocks) for blocks in rows]
    height = -(-(3 * conditions + experts) // 128) * 128
    width = cot.shape[1]
    return pl.pallas_call(
        functools.partial(sums_kernel, numbers, (conditions, experts)),
        out_shape=jax.ShapeDtypeStruct((height, width), f32),
        in_specs=[SMEM] + [VMEM] * (2 * sum(numbers) + 7),
        out_specs=VMEM,
        compiler_params=params(12),
        cost_estimate=cost(1e6, 1e4),
        name="table_sums",
    )(me, *rows[0], *rows[1], *backs[0], *backs[1], *lates, *stats, meta, cot, mix)


def grads_kernel(me_ref, near_ref, far_ref, *outs):
    width, half = outs[0].shape
    other_ref = outs[3]
    zero = ((0,), (0,))
    second = me_ref[2] != 0
    step = 256
    near, far = (late_views(ref, width, 2 * half) for ref in (near_ref, far_ref))
    for start in range(0, width, step):
        part = slice(start, start + step)
        for index, (left, right) in enumerate(((0, 2), (0, 3), (1, 4))):
            total = dot(near[left][:, part], near[right][...], zero)
            total += dot(far[left][:, part], far[right][...], zero)
            low, high = total[:, :half], total[:, half:]
            outs[index][part, :] = jnp.where(second, high, low).astype(bf16)
            other_ref[index, part, :] = jnp.where(second, low, high).astype(bf16)


def grads(me, lates, width, full):
    outs = pl.pallas_call(
        grads_kernel,
        out_shape=[jax.ShapeDtypeStruct((width, full // 2), bf16)] * 3
        + [jax.ShapeDtypeStruct((3, width, full // 2), bf16)],
        in_specs=[SMEM] + [VMEM] * 2,
        out_specs=[VMEM] * 4,
        compiler_params=params(12),
        cost_estimate=cost(1e6, 1e4),
        name="weight_grads",
    )(me, *lates)
    return outs[:3], outs[3]


def merge_kernel(count, cap, me_ref, meta_ref, *refs):
    picks = routing(me_ref[1], me_ref[0] - me_ref[1], meta_ref, count, cap).astype(bf16)
    rows = piece(refs[:-1], 0, count * cap, slice(None))
    refs[-1][...] = dot(picks, rows, ((0,), (0,))).astype(bf16)


def merge(me, meta, backs, cap):
    return pl.pallas_call(
        functools.partial(merge_kernel, len(backs), cap),
        out_shape=jax.ShapeDtypeStruct((meta.shape[1], backs[0].shape[1]), bf16),
        in_specs=[SMEM] + [VMEM] * (1 + len(backs)),
        out_specs=VMEM,
        compiler_params=params(8),
        cost_estimate=cost(1e9, 2e6),
        name="merge",
    )(me, meta, *backs)


def final_kernel(count, cap, me_ref, meta_ref, stamp_ref, tok_ref, cot_ref, table_ref, near_ref, far_ref, out_ref):
    picks = routing(me_ref[1], 0, meta_ref, count, cap).astype(bf16)
    mod_grad = dot(picks, near_ref[...], ((0,), (0,))) + far_ref[...].astype(f32)
    conditions = table_ref.shape[1]
    _, inverse, normed = normalize(tok_ref[...].astype(f32))
    pick = pick3((stamp_ref[:, 0:1] + 1).astype(f32), conditions)
    d_normed = mod_grad * (1.0 + dot(pick, split3(table_ref[1])))
    d_input = inverse * (
        d_normed
        - jnp.mean(d_normed, axis=-1, keepdims=True)
        - normed * jnp.mean(d_normed * normed, axis=-1, keepdims=True)
    )
    out_ref[...] = (cot_ref[...].astype(f32) + d_input).astype(bf16)


def final(me, meta, stamp_column, tokens, cot, table, near, far, count, cap):
    return pl.pallas_call(
        functools.partial(final_kernel, count, cap),
        out_shape=jax.ShapeDtypeStruct(tokens.shape, bf16),
        in_specs=[SMEM] + [VMEM] * 7,
        out_specs=VMEM,
        compiler_params=params(12),
        cost_estimate=cost(1e9, 4e6),
        name="final",
    )(me, meta, stamp_column, tokens, cot, table, near, far)


def rounded(values):
    return lax.reduce_precision(values, 8, 7)


def flip(values, name, size, bit):
    return lax.ppermute(values.astype(bf16), name, [(i, i ^ bit) for i in range(size)])


def scattered_axes(dp_axis, experts):
    return ([("dp", dp_axis, 1)] if dp_axis > 1 else []) + [("expert", experts, 1)]


def scatter_table(table, dp_axis, experts):
    for name, size, bit in scattered_axes(dp_axis, experts):
        high = (lax.axis_index(name) & bit) != 0
        rows = table.shape[0] // 2
        low_half, high_half = table[:rows], table[rows:]
        away = jnp.where(high, low_half, high_half)
        table = jnp.where(high, high_half, low_half)
        table = table + flip(away, name, size, bit).astype(f32)
    return table


def exchange_table(table, experts, first, last):
    bit = first
    while bit < last:
        table = rounded(table)
        table = table + flip(table, "expert", experts, bit).astype(f32)
        bit *= 2
    return table


def add_kernel(other_ref, *refs):
    number = len(refs) // 2
    for i in range(number):
        total = refs[i][...].astype(f32) + other_ref[i].astype(f32)
        refs[number + i][0] = total.astype(bf16)


def add(mine, other):
    width, half = mine[0].shape
    step = 256
    part = pl.BlockSpec((step, half), lambda i: (i, 0))
    return pl.pallas_call(
        add_kernel,
        grid=(width // step,),
        out_shape=[jax.ShapeDtypeStruct((1, width, half), bf16)] * len(mine),
        in_specs=[pl.BlockSpec((len(mine), step, half), lambda i: (0, i, 0))] + [part] * len(mine),
        out_specs=[pl.BlockSpec((1, step, half), lambda i: (0, i, 0))] * len(mine),
        compiler_params=params(12),
        cost_estimate=cost(1e6, 1e4),
        name="add",
    )(other, *mine)


def gather_table(table, dp_axis, experts):
    for name, size, bit in reversed(scattered_axes(dp_axis, experts)):
        high = (lax.axis_index(name) & bit) != 0
        other = flip(table, name, size, bit)
        table = jnp.concatenate(
            [jnp.where(high, other, table), jnp.where(high, table, other)], axis=0
        )
    return table


def local(experts, dp_axis, tokens, cotangent, mixture, stamp, expert_ids, modulation, router, w_gate, w_up, w_down):
    toks, width = tokens.shape
    conditions = modulation.shape[1]
    cap = min(toks, 4 * toks // experts)
    half = experts // 2
    index = lax.axis_index("expert").astype(jnp.int32)
    me = jnp.stack([index, index // half * half, lax.axis_index("dp").astype(jnp.int32)])
    halves = [list(range(half)), list(range(half, experts))]
    across = [(e, (e + half) % experts) for e in range(experts)]

    def hop(array):
        return lax.ppermute(array, "expert", across)

    def trade(array):
        blocks = array.reshape(half, cap, array.shape[1])
        blocks = lax.all_to_all(
            blocks, "expert", split_axis=0, concat_axis=0, tiled=True, axis_index_groups=halves
        )
        return blocks.reshape(array.shape)

    def fan(blocks):
        return [blocks[0]] + [
            lax.ppermute(blocks[k], "expert", [(e, e ^ k) for e in range(experts)])
            for k in range(1, half)
        ]

    def after(array, *others):
        return lax.optimization_barrier((array,) + others)[0]

    meta = jnp.concatenate(
        [expert_ids.T, stamp[None], jnp.zeros((5, toks), jnp.int32)], axis=0
    )
    gate, up, down = (
        lax.all_gather(w[0], "dp", axis=1, tiled=True) for w in (w_gate, w_up, w_down)
    )
    far_tokens = hop(tokens)
    far_meta = hop(meta)
    (near,) = pack(me, meta, [tokens, cotangent], True, False, half, cap)
    near, far_meta = lax.optimization_barrier((near, far_meta))
    near = trade(near)
    far_cot = hop(cotangent)
    far_cot, down = lax.optimization_barrier((far_cot, down))
    far = pack(me, far_meta, [far_tokens], True, True, half, cap)
    far_cots = pack(me, far_meta, [far_cot], False, True, half, cap)
    far = fan(far)
    near, kept = lax.optimization_barrier((near, far_cots[0]))
    far_cots = [kept] + list(far_cots[1:])
    far_cots = fan(far_cots)

    near_backs, near_late, near_stats = whole(me, [near], modulation, router, down, gate, up)
    near_late, far = lax.optimization_barrier((near_late, far))
    far_in = forward(me, far, modulation, router, gate, up)
    far_backs, far_late, far_stats = backward(
        me, far_cots, modulation, router, *far_in, down, gate, up
    )
    far_back = fan(far_backs)
    lates = [near_late, far_late]
    table = sums(
        me, [[near], far], [near_backs, far_backs], lates, [near_stats, far_stats],
        meta, cotangent, mixture, conditions, experts,
    )
    mine, other = grads(me, lates, *gate.shape)
    merged = merge(me, far_meta, far_back, cap)
    merged, table, other, near_back = lax.optimization_barrier(
        (merged, table, other, near_backs[0])
    )
    far_grad = hop(merged)
    near_back = trade(near_back)
    other = lax.ppermute(other, "dp", [(i, dp_axis - 1 - i) for i in range(dp_axis)])
    table = scatter_table(table, dp_axis, experts)
    table = exchange_table(table, experts, 2, 2)
    d_gate, d_up, d_down = add(mine, other)
    table, near_back, far_grad, d_gate, d_up, d_down = lax.optimization_barrier(
        (table, near_back, far_grad, d_gate, d_up, d_down)
    )
    table = rounded(exchange_table(table, experts, 2, experts)).astype(bf16)
    table = gather_table(table, dp_axis, experts)
    d_tokens = final(
        me, meta, stamp[:, None], tokens, cotangent, modulation, near_back, far_grad, half, cap
    )
    table, d_tokens = lax.optimization_barrier((table, d_tokens))
    table = table.astype(f32)
    d_modulation = table[: 3 * conditions].reshape(3, conditions, width)
    d_router = table[3 * conditions : 3 * conditions + experts]
    return (d_tokens, d_gate, d_up, d_down, d_router, d_modulation)


def solution(mesh):
    return jax.shard_map(
        functools.partial(local, mesh.shape["expert"], mesh.shape["dp"]),
        mesh=mesh,
        in_specs=(
            P(("groups", "expert", "dp"), None),
            P(("groups", "expert", "dp"), None),
            P(("groups", "expert", "dp"), None),
            P(("groups", "expert", "dp")),
            P(("groups", "expert", "dp"), None),
            P(),
            P(),
            P("expert", None, "dp"),
            P("expert", None, "dp"),
            P("expert", None, "dp"),
        ),
        out_specs=(
            P(("groups", "expert", "dp"), None),
            P(("groups", "expert"), None, "dp"),
            P(("groups", "expert"), None, "dp"),
            P(("groups", "expert"), None, "dp"),
            P("groups", None),
            P(None, "groups", None),
        ),
        check_vma=False,
    )
```

```python
import functools

import jax
import jax.numpy as jnp
from jax import lax
from jax.experimental import pallas as pl
from jax.experimental.pallas import tpu as pltpu
from jax.sharding import PartitionSpec as P

epsilon = 1e-06
f32 = jnp.float32
bf16 = jnp.bfloat16
LANES = 128
VMEM = pl.BlockSpec(memory_space=pltpu.VMEM)
SMEM = pl.BlockSpec(memory_space=pltpu.SMEM)


def params(mib):
    return pltpu.CompilerParams(vmem_limit_bytes=mib * 1024 * 1024)


def cost(flops, moved):
    return pl.CostEstimate(flops=int(flops), bytes_accessed=int(moved), transcendentals=0)


def dot(a, b, dims=((1,), (0,))):
    return lax.dot_general(a, b, (dims, ((), ())), preferred_element_type=f32)


def routing(base, flip, meta_ref, count, cap):
    toks = meta_ref.shape[1]
    height = max(8, count)
    wanted = base + jnp.bitwise_xor(
        flip, lax.broadcasted_iota(jnp.int32, (height, toks), 0)
    )
    member = jnp.logical_or(meta_ref[0:1, :] == wanted, meta_ref[1:2, :] == wanted)
    earlier = lax.broadcasted_iota(jnp.int32, (toks, toks), 0) < lax.broadcasted_iota(
        jnp.int32, (toks, toks), 1
    )
    slots = dot(member.astype(f32).astype(bf16), earlier.astype(f32).astype(bf16))
    slots = jnp.where(member, slots, -1.0).astype(jnp.int32)
    place = lax.broadcasted_iota(jnp.int32, (cap, toks), 0)
    picks = [(slots[k : k + 1, :] == place).astype(f32) for k in range(count)]
    return jnp.concatenate(picks, axis=0)


def split3(table):
    high = table.astype(bf16)
    rest = table - high.astype(f32)
    middle = rest.astype(bf16)
    low = (rest - middle.astype(f32)).astype(bf16)
    return jnp.concatenate([high, middle, low], axis=0)


def pick3(column, conditions):
    lane = lax.broadcasted_iota(jnp.int32, (column.shape[0], 3 * conditions), 1)
    return (lax.rem(lane, conditions) + 1 == column.astype(jnp.int32)).astype(f32).astype(bf16)


def own_row(me, router_ref):
    table = router_ref[...].astype(f32)
    place = lax.broadcasted_iota(jnp.int32, table.shape, 0)
    return jnp.sum(jnp.where(place == me, table, 0.0), axis=0, keepdims=True)


def normalize(values):
    mean = jnp.mean(values, axis=-1, keepdims=True)
    centred = values - mean
    inverse = lax.rsqrt(jnp.mean(centred * centred, axis=-1, keepdims=True) + epsilon)
    return mean, inverse, centred * inverse


def piece(refs, start, size, columns):
    height = refs[0].shape[0]
    if size <= height:
        block, row = divmod(start, height)
        return refs[block][row : row + size, columns]
    parts = [refs[start // height + i][:, columns] for i in range(size // height)]
    return jnp.concatenate(parts, axis=0)


def put(refs, start, values, columns):
    height = refs[0].shape[0]
    size = values.shape[0]
    if size <= height:
        block, row = divmod(start, height)
        refs[block][row : row + size, columns] = values
    else:
        for i in range(size // height):
            refs[start // height + i][:, columns] = values[i * height : (i + 1) * height]


def pack_kernel(count, cap, number, flipped, stamped, me_ref, meta_ref, *refs):
    arrays, outs = refs[:number], refs[number:]
    flip = me_ref[0] - me_ref[1] if flipped else 0
    picks = routing(me_ref[1], flip, meta_ref, count, cap)
    whole = picks.astype(bf16)
    total = count * cap
    width = arrays[0].shape[1]
    put(outs, 0, dot(whole, arrays[0][...]).astype(bf16), slice(0, width))
    at = width
    if stamped:
        column = jnp.sum(picks * (meta_ref[2:3, :] + 1).astype(f32), axis=1, keepdims=True)
        put(outs, 0, jnp.broadcast_to(column, (total, LANES)).astype(bf16), slice(at, at + LANES))
        at += LANES
    for array in arrays[1:]:
        put(outs, 0, dot(whole, array[...]).astype(bf16), slice(at, at + width))
        at += width


def pack(me, meta, arrays, stamped, flipped, count, cap):
    width = arrays[0].shape[1] * len(arrays) + (LANES if stamped else 0)
    shape = (cap, width) if flipped else (count * cap, width)
    number = count if flipped else 1
    return pl.pallas_call(
        functools.partial(pack_kernel, count, cap, len(arrays), flipped, stamped),
        out_shape=[jax.ShapeDtypeStruct(shape, bf16)] * number,
        in_specs=[SMEM] + [VMEM] * (1 + len(arrays)),
        out_specs=[VMEM] * number,
        compiler_params=params(8),
        cost_estimate=cost(1e9, 4e6),
        name="pack",
    )(me, meta, *arrays)


def late_views(late_ref, width, full):
    edges = [0, width, 2 * width, 2 * width + full, 2 * width + 2 * full, 2 * width + 3 * full]
    return [late_ref.at[:, low:high] for low, high in zip(edges, edges[1:])]


def forward_body(me_ref, ins, table_ref, router_ref, gate_ref, up_ref, mod_ref, stats_ref, act_ref, fac_ref, hid_ref):
    count, width = mod_ref.shape
    full = gate_ref.shape[1]
    conditions = table_ref.shape[1]
    chunk = 64
    shift_parts, scale_parts = split3(table_ref[0]), split3(table_ref[1])
    router_row = own_row(me_ref[0], router_ref)
    lane = lax.broadcasted_iota(jnp.int32, (chunk, LANES), 1)
    for start in range(0, count, chunk):
        part = slice(start, start + chunk)
        mean, inverse, normed = normalize(piece(ins, start, chunk, slice(0, width)).astype(f32))
        mark = piece(ins, start, chunk, slice(width, width + 1)).astype(f32)
        pick = pick3(mark, conditions)
        rows = (normed * (1.0 + dot(pick, scale_parts)) + dot(pick, shift_parts)).astype(bf16)
        mod_ref[part, :] = rows
        logit = jnp.sum(rows.astype(f32) * router_row, axis=1, keepdims=True)
        prob = jax.nn.sigmoid(logit)
        stats_ref[part, :] = jnp.where(
            lane == 0, mean, jnp.where(lane == 1, inverse, jnp.where(lane == 2, prob, mark))
        )
    step = 256
    for start in range(0, full, step):
        columns = slice(start, start + step)
        pre_gate = dot(mod_ref[...], gate_ref[:, columns])
        pre_up = dot(mod_ref[...], up_ref[:, columns])
        sig = jax.nn.sigmoid(pre_gate)
        active = pre_gate * sig
        act_ref[:, columns] = active
        fac_ref[:, columns] = pre_up * sig * (1.0 + pre_gate * (1.0 - sig))
        hid_ref[:, columns] = (active * pre_up).astype(bf16)


def backward_body(offset, me_ref, cots, table_ref, router_ref, stats_ref, act_ref, fac_ref, hid_ref, down_ref, gate_ref, up_ref, backs, og_ref, gg_ref, ug_ref, lg_ref, ups_ref):
    count, width = og_ref.shape
    full = gate_ref.shape[1]
    conditions = table_ref.shape[1]
    gate_parts = split3(table_ref[2])
    prob = stats_ref[:, 2:3]
    chunk = 64
    for start in range(0, count, chunk):
        part = slice(start, start + chunk)
        pick = pick3(stats_ref[part, 3:4], conditions)
        cot = piece(cots, start, chunk, slice(offset, offset + width)).astype(f32)
        upstream = (dot(pick, gate_parts) * cot).astype(bf16)
        ups_ref[part, :] = upstream
        og_ref[part, :] = (stats_ref[part, 2:3] * upstream.astype(f32)).astype(bf16)
    prob_grad = jnp.zeros((count, 1), f32)
    step = 256
    for start in range(0, full, step):
        columns = slice(start, start + step)
        raw = dot(ups_ref[...], down_ref[:, columns])
        prob_grad += jnp.sum(hid_ref[:, columns].astype(f32) * raw, axis=1, keepdims=True)
        hidden_grad = prob * raw
        gg_ref[:, columns] = (hidden_grad * fac_ref[:, columns]).astype(bf16)
        ug_ref[:, columns] = (hidden_grad * act_ref[:, columns]).astype(bf16)
    logit_grad = prob_grad * prob * (1.0 - prob)
    lane = lax.broadcasted_iota(jnp.int32, stats_ref.shape, 1)
    lg_ref[...] = jnp.where(lane == 4, logit_grad, stats_ref[...])
    router_row = own_row(me_ref[0], router_ref)
    for start in range(0, width, step):
        part = slice(start, start + step)
        total = dot(gg_ref[...], gate_ref[part, :], ((1,), (1,)))
        total += dot(ug_ref[...], up_ref[part, :], ((1,), (1,)))
        put(backs, 0, (total + logit_grad * router_row[:, part]).astype(bf16), part)


def forward_kernel(number, me_ref, *refs):
    forward_body(me_ref, refs[:number], *refs[number:])


def forward(me, blocks, table, router, gate, up):
    count = sum(block.shape[0] for block in blocks)
    width, full = gate.shape
    wide = jax.ShapeDtypeStruct((count, full), f32)
    return pl.pallas_call(
        functools.partial(forward_kernel, len(blocks)),
        out_shape=[
            jax.ShapeDtypeStruct((count, width), bf16),
            jax.ShapeDtypeStruct((count, LANES), f32),
            wide,
            wide,
            jax.ShapeDtypeStruct((count, full), bf16),
        ],
        in_specs=[SMEM] + [VMEM] * (len(blocks) + 4),
        out_specs=[VMEM] * 5,
        compiler_params=params(12),
        cost_estimate=cost(4 * count * width * full, 4 * width * full + count * 12000),
        name="expert_in",
    )(me, *blocks, table, router, gate, up)


def backward_shapes(blocks, width, full):
    count = sum(block.shape[0] for block in blocks)
    return [jax.ShapeDtypeStruct((block.shape[0], width), bf16) for block in blocks] + [
        jax.ShapeDtypeStruct((count, 2 * width + 3 * full), bf16),
        jax.ShapeDtypeStruct((count, LANES), f32),
    ]


def backward_kernel(number, me_ref, *refs):
    cots, refs = refs[:number], refs[number:]
    table_ref, router_ref, seen_ref, stats_ref, act_ref, fac_ref, hid_ref, down_ref, gate_ref, up_ref = refs[:10]
    backs, (late_ref, lg_ref, ups_ref) = refs[10 : 10 + number], refs[10 + number :]
    mod, og, gg, ug, hid = late_views(late_ref, *gate_ref.shape)
    backward_body(0, me_ref, cots, table_ref, router_ref, stats_ref, act_ref, fac_ref, hid_ref, down_ref, gate_ref, up_ref, backs, og, gg, ug, lg_ref, ups_ref)
    mod[...] = seen_ref[...]
    hid[...] = hid_ref[...]


def backward(me, blocks, table, router, mod, stats, act, fac, hid, down, gate, up):
    count = sum(block.shape[0] for block in blocks)
    width, full = gate.shape
    number = len(blocks)
    outs = pl.pallas_call(
        functools.partial(backward_kernel, number),
        out_shape=backward_shapes(blocks, width, full),
        in_specs=[SMEM] + [VMEM] * (number + 10),
        out_specs=[VMEM] * (number + 2),
        scratch_shapes=[pltpu.VMEM((count, width), bf16)],
        compiler_params=params(12),
        cost_estimate=cost(6 * count * width * full, 6 * width * full + count * 16000),
        name="expert_back",
    )(me, *blocks, table, router, mod, stats, act, fac, hid, down, gate, up)
    return outs[:number], *outs[number:]


def whole_kernel(number, me_ref, *refs):
    blocks, refs = refs[:number], refs[number:]
    table_ref, router_ref, down_ref, gate_ref, up_ref = refs[:5]
    backs, refs = refs[5 : 5 + number], refs[5 + number :]
    late_ref, lg_ref, stats_ref, act_ref, fac_ref, ups_ref = refs
    mod, og, gg, ug, hid = late_views(late_ref, *gate_ref.shape)
    forward_body(me_ref, blocks, table_ref, router_ref, gate_ref, up_ref, mod, stats_ref, act_ref, fac_ref, hid)
    backward_body(mod.shape[1] + LANES, me_ref, blocks, table_ref, router_ref, stats_ref, act_ref, fac_ref, hid, down_ref, gate_ref, up_ref, backs, og, gg, ug, lg_ref, ups_ref)


def whole(me, blocks, table, router, down, gate, up):
    count = sum(block.shape[0] for block in blocks)
    width, full = gate.shape
    number = len(blocks)
    outs = pl.pallas_call(
        functools.partial(whole_kernel, number),
        out_shape=backward_shapes(blocks, width, full),
        in_specs=[SMEM] + [VMEM] * (number + 5),
        out_specs=[VMEM] * (number + 2),
        scratch_shapes=[pltpu.VMEM((count, LANES), f32)]
        + [pltpu.VMEM((count, full), f32)] * 2
        + [pltpu.VMEM((count, width), bf16)],
        compiler_params=params(16),
        cost_estimate=cost(10 * count * width * full, 6 * width * full + count * 16000),
        name="expert_whole",
    )(me, *blocks, table, router, down, gate, up)
    return outs[:number], *outs[number:]


def sums_kernel(numbers, tall, me_ref, *refs):
    rows, backs = [], []
    for group in (rows, backs):
        for number in numbers:
            group.append(refs[:number])
            refs = refs[number:]
    lates, stats = refs[:2], refs[2:4]
    meta_ref, cot_ref, mix_ref, out_ref = refs[4:]
    count, width = lates[0].shape[0], cot_ref.shape[1]
    conditions, experts = tall
    zero = ((0,), (0,))
    shift_sum = jnp.zeros((conditions, width), f32)
    scale_sum = jnp.zeros((conditions, width), f32)
    router_sum = jnp.zeros((1, width), f32)
    chunk = 128
    for q in range(2):
        for start in range(0, count, chunk):
            part = slice(start, start + chunk)
            lane = lax.broadcasted_iota(jnp.int32, (chunk, conditions), 1)
            mark = stats[q][part, 3:4].astype(jnp.int32)
            pick = (lane + 1 == mark).astype(f32).astype(bf16)
            back = piece(backs[q], start, chunk, slice(0, width))
            mean, inverse = stats[q][part, 0:1], stats[q][part, 1:2]
            values = piece(rows[q], start, chunk, slice(0, width)).astype(f32)
            normed = (values - mean) * inverse
            product = back.astype(f32) * normed
            high = product.astype(bf16)
            low = (product - high.astype(f32)).astype(bf16)
            shift_sum += dot(pick, back, zero)
            scale_sum += dot(pick, high, zero) + dot(pick, low, zero)
            weighted = stats[q][part, 4:5] * lates[q][part, :width].astype(f32)
            router_sum += jnp.sum(weighted, axis=0, keepdims=True)
    toks = cot_ref.shape[0]
    wanted = lax.broadcasted_iota(jnp.int32, (conditions, toks), 0)
    pick = (meta_ref[2:3, :] == wanted).astype(f32).astype(bf16)
    product = cot_ref[...].astype(f32) * mix_ref[...].astype(f32)
    high = product.astype(bf16)
    low = (product - high.astype(f32)).astype(bf16)
    out_ref[0:conditions, :] = shift_sum
    out_ref[conditions : 2 * conditions, :] = scale_sum
    out_ref[2 * conditions : 3 * conditions, :] = dot(pick, high) + dot(pick, low)
    place = lax.broadcasted_iota(jnp.int32, (out_ref.shape[0] - 3 * conditions, width), 0)
    out_ref[3 * conditions :, :] = jnp.where(place == me_ref[0], router_sum, 0.0)


def sums(me, rows, backs, lates, stats, meta, cot, mix, conditions, experts):
    numbers = [len(blocks) for blocks in rows]
    height = -(-(3 * conditions + experts) // 128) * 128
    width = cot.shape[1]
    return pl.pallas_call(
        functools.partial(sums_kernel, numbers, (conditions, experts)),
        out_shape=jax.ShapeDtypeStruct((height, width), f32),
        in_specs=[SMEM] + [VMEM] * (2 * sum(numbers) + 7),
        out_specs=VMEM,
        compiler_params=params(12),
        cost_estimate=cost(1e6, 1e4),
        name="table_sums",
    )(me, *rows[0], *rows[1], *backs[0], *backs[1], *lates, *stats, meta, cot, mix)


def grads_kernel(me_ref, near_ref, far_ref, *outs):
    width, half = outs[0].shape
    other_ref = outs[3]
    zero = ((0,), (0,))
    second = me_ref[2] != 0
    step = 256
    near, far = (late_views(ref, width, 2 * half) for ref in (near_ref, far_ref))
    for start in range(0, width, step):
        part = slice(start, start + step)
        for index, (left, right) in enumerate(((0, 2), (0, 3), (1, 4))):
            total = dot(near[left][:, part], near[right][...], zero)
            total += dot(far[left][:, part], far[right][...], zero)
            low, high = total[:, :half], total[:, half:]
            outs[index][part, :] = jnp.where(second, high, low).astype(bf16)
            other_ref[index, part, :] = jnp.where(second, low, high).astype(bf16)


def grads(me, lates, width, full):
    outs = pl.pallas_call(
        grads_kernel,
        out_shape=[jax.ShapeDtypeStruct((width, full // 2), bf16)] * 3
        + [jax.ShapeDtypeStruct((3, width, full // 2), bf16)],
        in_specs=[SMEM] + [VMEM] * 2,
        out_specs=[VMEM] * 4,
        compiler_params=params(12),
        cost_estimate=cost(1e6, 1e4),
        name="weight_grads",
    )(me, *lates)
    return outs[:3], outs[3]


def merge_kernel(count, cap, me_ref, meta_ref, *refs):
    picks = routing(me_ref[1], me_ref[0] - me_ref[1], meta_ref, count, cap).astype(bf16)
    rows = piece(refs[:-1], 0, count * cap, slice(None))
    refs[-1][...] = dot(picks, rows, ((0,), (0,))).astype(bf16)


def merge(me, meta, backs, cap):
    return pl.pallas_call(
        functools.partial(merge_kernel, len(backs), cap),
        out_shape=jax.ShapeDtypeStruct((meta.shape[1], backs[0].shape[1]), bf16),
        in_specs=[SMEM] + [VMEM] * (1 + len(backs)),
        out_specs=VMEM,
        compiler_params=params(8),
        cost_estimate=cost(1e9, 2e6),
        name="merge",
    )(me, meta, *backs)


def final_kernel(count, cap, me_ref, meta_ref, stamp_ref, tok_ref, cot_ref, table_ref, near_ref, far_ref, out_ref):
    picks = routing(me_ref[1], 0, meta_ref, count, cap).astype(bf16)
    mod_grad = dot(picks, near_ref[...], ((0,), (0,))) + far_ref[...].astype(f32)
    conditions = table_ref.shape[1]
    _, inverse, normed = normalize(tok_ref[...].astype(f32))
    pick = pick3((stamp_ref[:, 0:1] + 1).astype(f32), conditions)
    d_normed = mod_grad * (1.0 + dot(pick, split3(table_ref[1])))
    d_input = inverse * (
        d_normed
        - jnp.mean(d_normed, axis=-1, keepdims=True)
        - normed * jnp.mean(d_normed * normed, axis=-1, keepdims=True)
    )
    out_ref[...] = (cot_ref[...].astype(f32) + d_input).astype(bf16)


def final(me, meta, stamp_column, tokens, cot, table, near, far, count, cap):
    return pl.pallas_call(
        functools.partial(final_kernel, count, cap),
        out_shape=jax.ShapeDtypeStruct(tokens.shape, bf16),
        in_specs=[SMEM] + [VMEM] * 7,
        out_specs=VMEM,
        compiler_params=params(12),
        cost_estimate=cost(1e9, 4e6),
        name="final",
    )(me, meta, stamp_column, tokens, cot, table, near, far)


def rounded(values):
    return lax.reduce_precision(values, 8, 7)


def flip(values, name, size, bit):
    return lax.ppermute(values.astype(bf16), name, [(i, i ^ bit) for i in range(size)])


def scattered_axes(dp_axis, experts):
    return ([("dp", dp_axis, 1)] if dp_axis > 1 else []) + [("expert", experts, 1)]


def scatter_table(table, dp_axis, experts):
    for name, size, bit in scattered_axes(dp_axis, experts):
        high = (lax.axis_index(name) & bit) != 0
        rows = table.shape[0] // 2
        low_half, high_half = table[:rows], table[rows:]
        away = jnp.where(high, low_half, high_half)
        table = jnp.where(high, high_half, low_half)
        table = table + flip(away, name, size, bit).astype(f32)
    return table


def exchange_table(table, experts, first, last):
    bit = first
    while bit < last:
        table = rounded(table)
        table = table + flip(table, "expert", experts, bit).astype(f32)
        bit *= 2
    return table


def add_kernel(other_ref, *refs):
    number = len(refs) // 2
    for i in range(number):
        total = refs[i][...].astype(f32) + other_ref[i].astype(f32)
        refs[number + i][0] = total.astype(bf16)


def add(mine, other):
    width, half = mine[0].shape
    step = 256
    part = pl.BlockSpec((step, half), lambda i: (i, 0))
    return pl.pallas_call(
        add_kernel,
        grid=(width // step,),
        out_shape=[jax.ShapeDtypeStruct((1, width, half), bf16)] * len(mine),
        in_specs=[pl.BlockSpec((len(mine), step, half), lambda i: (0, i, 0))] + [part] * len(mine),
        out_specs=[pl.BlockSpec((1, step, half), lambda i: (0, i, 0))] * len(mine),
        compiler_params=params(12),
        cost_estimate=cost(1e6, 1e4),
        name="add",
    )(other, *mine)


def gather_table(table, dp_axis, experts):
    for name, size, bit in reversed(scattered_axes(dp_axis, experts)):
        high = (lax.axis_index(name) & bit) != 0
        other = flip(table, name, size, bit)
        table = jnp.concatenate(
            [jnp.where(high, other, table), jnp.where(high, table, other)], axis=0
        )
    return table


def local(experts, dp_axis, tokens, cotangent, mixture, stamp, expert_ids, modulation, router, w_gate, w_up, w_down):
    toks, width = tokens.shape
    conditions = modulation.shape[1]
    cap = min(toks, 4 * toks // experts)
    half = experts // 2
    index = lax.axis_index("expert").astype(jnp.int32)
    me = jnp.stack([index, index // half * half, lax.axis_index("dp").astype(jnp.int32)])
    halves = [list(range(half)), list(range(half, experts))]
    across = [(e, (e + half) % experts) for e in range(experts)]

    def hop(array):
        return lax.ppermute(array, "expert", across)

    def trade(array):
        blocks = array.reshape(half, cap, array.shape[1])
        blocks = lax.all_to_all(
            blocks, "expert", split_axis=0, concat_axis=0, tiled=True, axis_index_groups=halves
        )
        return blocks.reshape(array.shape)

    def fan(blocks):
        return [blocks[0]] + [
            lax.ppermute(blocks[k], "expert", [(e, e ^ k) for e in range(experts)])
            for k in range(1, half)
        ]

    def after(array, *others):
        return lax.optimization_barrier((array,) + others)[0]

    meta = jnp.concatenate(
        [expert_ids.T, stamp[None], jnp.zeros((5, toks), jnp.int32)], axis=0
    )
    gate, up, down = (
        lax.all_gather(w[0], "dp", axis=1, tiled=True) for w in (w_gate, w_up, w_down)
    )
    far_tokens = hop(tokens)
    far_meta = hop(meta)
    (near,) = pack(me, meta, [tokens, cotangent], True, False, half, cap)
    near, far_meta = lax.optimization_barrier((near, far_meta))
    near = trade(near)
    far_cot = hop(cotangent)
    far = pack(me, far_meta, [far_tokens], True, True, half, cap)
    far_cots = pack(me, far_meta, [far_cot], False, True, half, cap)
    far = fan(far)
    near, kept = lax.optimization_barrier((near, far_cots[0]))
    far_cots = [kept] + list(far_cots[1:])
    far_cots = fan(far_cots)

    near_backs, near_late, near_stats = whole(me, [near], modulation, router, down, gate, up)
    near_late, far = lax.optimization_barrier((near_late, far))
    far_in = forward(me, far, modulation, router, gate, up)
    far_backs, far_late, far_stats = backward(
        me, far_cots, modulation, router, *far_in, down, gate, up
    )
    far_back = fan(far_backs)
    lates = [near_late, far_late]
    table = sums(
        me, [[near], far], [near_backs, far_backs], lates, [near_stats, far_stats],
        meta, cotangent, mixture, conditions, experts,
    )
    mine, other = grads(me, lates, *gate.shape)
    merged = merge(me, far_meta, far_back, cap)
    merged, table, other, near_back = lax.optimization_barrier(
        (merged, table, other, near_backs[0])
    )
    far_grad = hop(merged)
    near_back = trade(near_back)
    other = lax.ppermute(other, "dp", [(i, dp_axis - 1 - i) for i in range(dp_axis)])
    table = scatter_table(table, dp_axis, experts)
    table = exchange_table(table, experts, 2, 2)
    d_gate, d_up, d_down = add(mine, other)
    table, near_back, far_grad, d_gate, d_up, d_down = lax.optimization_barrier(
        (table, near_back, far_grad, d_gate, d_up, d_down)
    )
    table = rounded(exchange_table(table, experts, 2, experts)).astype(bf16)
    table = gather_table(table, dp_axis, experts)
    d_tokens = final(
        me, meta, stamp[:, None], tokens, cotangent, modulation, near_back, far_grad, half, cap
    )
    table, d_tokens = lax.optimization_barrier((table, d_tokens))
    table = table.astype(f32)
    d_modulation = table[: 3 * conditions].reshape(3, conditions, width)
    d_router = table[3 * conditions : 3 * conditions + experts]
    return (d_tokens, d_gate, d_up, d_down, d_router, d_modulation)


def solution(mesh):
    return jax.shard_map(
        functools.partial(local, mesh.shape["expert"], mesh.shape["dp"]),
        mesh=mesh,
        in_specs=(
            P(("groups", "expert", "dp"), None),
            P(("groups", "expert", "dp"), None),
            P(("groups", "expert", "dp"), None),
            P(("groups", "expert", "dp")),
            P(("groups", "expert", "dp"), None),
            P(),
            P(),
            P("expert", None, "dp"),
            P("expert", None, "dp"),
            P("expert", None, "dp"),
        ),
        out_specs=(
            P(("groups", "expert", "dp"), None),
            P(("groups", "expert"), None, "dp"),
            P(("groups", "expert"), None, "dp"),
            P(("groups", "expert"), None, "dp"),
            P("groups", None),
            P(None, "groups", None),
        ),
        check_vma=False,
    )
```

```python
import functools

import jax
import jax.numpy as jnp
from jax import lax
from jax.experimental import pallas as pl
from jax.experimental.pallas import tpu as pltpu
from jax.sharding import PartitionSpec as P

epsilon = 1e-06
f32 = jnp.float32
bf16 = jnp.bfloat16
LANES = 128
VMEM = pl.BlockSpec(memory_space=pltpu.VMEM)
SMEM = pl.BlockSpec(memory_space=pltpu.SMEM)


def params(mib):
    return pltpu.CompilerParams(vmem_limit_bytes=mib * 1024 * 1024)


def cost(flops, moved):
    return pl.CostEstimate(flops=int(flops), bytes_accessed=int(moved), transcendentals=0)


def dot(a, b, dims=((1,), (0,))):
    return lax.dot_general(a, b, (dims, ((), ())), preferred_element_type=f32)


def routing(base, flip, meta_ref, count, cap):
    toks = meta_ref.shape[1]
    height = max(8, count)
    wanted = base + jnp.bitwise_xor(
        flip, lax.broadcasted_iota(jnp.int32, (height, toks), 0)
    )
    member = jnp.logical_or(meta_ref[0:1, :] == wanted, meta_ref[1:2, :] == wanted)
    earlier = lax.broadcasted_iota(jnp.int32, (toks, toks), 0) < lax.broadcasted_iota(
        jnp.int32, (toks, toks), 1
    )
    slots = dot(member.astype(f32).astype(bf16), earlier.astype(f32).astype(bf16))
    slots = jnp.where(member, slots, -1.0).astype(jnp.int32)
    place = lax.broadcasted_iota(jnp.int32, (cap, toks), 0)
    picks = [(slots[k : k + 1, :] == place).astype(f32) for k in range(count)]
    return jnp.concatenate(picks, axis=0)


def split3(table):
    high = table.astype(bf16)
    rest = table - high.astype(f32)
    middle = rest.astype(bf16)
    low = (rest - middle.astype(f32)).astype(bf16)
    return jnp.concatenate([high, middle, low], axis=0)


def pick3(column, conditions):
    lane = lax.broadcasted_iota(jnp.int32, (column.shape[0], 3 * conditions), 1)
    return (lax.rem(lane, conditions) + 1 == column.astype(jnp.int32)).astype(f32).astype(bf16)


def own_row(me, router_ref):
    table = router_ref[...].astype(f32)
    place = lax.broadcasted_iota(jnp.int32, table.shape, 0)
    return jnp.sum(jnp.where(place == me, table, 0.0), axis=0, keepdims=True)


def normalize(values):
    mean = jnp.mean(values, axis=-1, keepdims=True)
    centred = values - mean
    inverse = lax.rsqrt(jnp.mean(centred * centred, axis=-1, keepdims=True) + epsilon)
    return mean, inverse, centred * inverse


def piece(refs, start, size, columns):
    height = refs[0].shape[0]
    if size <= height:
        block, row = divmod(start, height)
        return refs[block][row : row + size, columns]
    parts = [refs[start // height + i][:, columns] for i in range(size // height)]
    return jnp.concatenate(parts, axis=0)


def put(refs, start, values, columns):
    height = refs[0].shape[0]
    size = values.shape[0]
    if size <= height:
        block, row = divmod(start, height)
        refs[block][row : row + size, columns] = values
    else:
        for i in range(size // height):
            refs[start // height + i][:, columns] = values[i * height : (i + 1) * height]


def pack_kernel(count, cap, number, flipped, stamped, me_ref, meta_ref, *refs):
    arrays, outs = refs[:number], refs[number:]
    flip = me_ref[0] - me_ref[1] if flipped else 0
    picks = routing(me_ref[1], flip, meta_ref, count, cap)
    whole = picks.astype(bf16)
    total = count * cap
    width = arrays[0].shape[1]
    put(outs, 0, dot(whole, arrays[0][...]).astype(bf16), slice(0, width))
    at = width
    if stamped:
        column = jnp.sum(picks * (meta_ref[2:3, :] + 1).astype(f32), axis=1, keepdims=True)
        put(outs, 0, jnp.broadcast_to(column, (total, LANES)).astype(bf16), slice(at, at + LANES))
        at += LANES
    for array in arrays[1:]:
        put(outs, 0, dot(whole, array[...]).astype(bf16), slice(at, at + width))
        at += width


def pack(me, meta, arrays, stamped, flipped, count, cap):
    width = arrays[0].shape[1] * len(arrays) + (LANES if stamped else 0)
    shape = (cap, width) if flipped else (count * cap, width)
    number = count if flipped else 1
    return pl.pallas_call(
        functools.partial(pack_kernel, count, cap, len(arrays), flipped, stamped),
        out_shape=[jax.ShapeDtypeStruct(shape, bf16)] * number,
        in_specs=[SMEM] + [VMEM] * (1 + len(arrays)),
        out_specs=[VMEM] * number,
        compiler_params=params(8),
        cost_estimate=cost(1e9, 4e6),
        name="pack",
    )(me, meta, *arrays)


def late_views(late_ref, width, full):
    edges = [0, width, 2 * width, 2 * width + full, 2 * width + 2 * full, 2 * width + 3 * full]
    return [late_ref.at[:, low:high] for low, high in zip(edges, edges[1:])]


def forward_body(me_ref, ins, table_ref, router_ref, gate_ref, up_ref, mod_ref, stats_ref, act_ref, fac_ref, hid_ref):
    count, width = mod_ref.shape
    full = gate_ref.shape[1]
    conditions = table_ref.shape[1]
    chunk = 64
    shift_parts, scale_parts = split3(table_ref[0]), split3(table_ref[1])
    router_row = own_row(me_ref[0], router_ref)
    lane = lax.broadcasted_iota(jnp.int32, (chunk, LANES), 1)
    for start in range(0, count, chunk):
        part = slice(start, start + chunk)
        mean, inverse, normed = normalize(piece(ins, start, chunk, slice(0, width)).astype(f32))
        mark = piece(ins, start, chunk, slice(width, width + 1)).astype(f32)
        pick = pick3(mark, conditions)
        rows = (normed * (1.0 + dot(pick, scale_parts)) + dot(pick, shift_parts)).astype(bf16)
        mod_ref[part, :] = rows
        logit = jnp.sum(rows.astype(f32) * router_row, axis=1, keepdims=True)
        prob = jax.nn.sigmoid(logit)
        stats_ref[part, :] = jnp.where(
            lane == 0, mean, jnp.where(lane == 1, inverse, jnp.where(lane == 2, prob, mark))
        )
    step = 256
    for start in range(0, full, step):
        columns = slice(start, start + step)
        pre_gate = dot(mod_ref[...], gate_ref[:, columns])
        pre_up = dot(mod_ref[...], up_ref[:, columns])
        sig = jax.nn.sigmoid(pre_gate)
        active = pre_gate * sig
        act_ref[:, columns] = active
        fac_ref[:, columns] = pre_up * sig * (1.0 + pre_gate * (1.0 - sig))
        hid_ref[:, columns] = (active * pre_up).astype(bf16)


def backward_body(offset, me_ref, cots, table_ref, router_ref, stats_ref, act_ref, fac_ref, hid_ref, down_ref, gate_ref, up_ref, backs, og_ref, gg_ref, ug_ref, lg_ref, ups_ref):
    count, width = og_ref.shape
    full = gate_ref.shape[1]
    conditions = table_ref.shape[1]
    gate_parts = split3(table_ref[2])
    prob = stats_ref[:, 2:3]
    chunk = 64
    for start in range(0, count, chunk):
        part = slice(start, start + chunk)
        pick = pick3(stats_ref[part, 3:4], conditions)
        cot = piece(cots, start, chunk, slice(offset, offset + width)).astype(f32)
        upstream = (dot(pick, gate_parts) * cot).astype(bf16)
        ups_ref[part, :] = upstream
        og_ref[part, :] = (stats_ref[part, 2:3] * upstream.astype(f32)).astype(bf16)
    prob_grad = jnp.zeros((count, 1), f32)
    step = 256
    for start in range(0, full, step):
        columns = slice(start, start + step)
        raw = dot(ups_ref[...], down_ref[:, columns])
        prob_grad += jnp.sum(hid_ref[:, columns].astype(f32) * raw, axis=1, keepdims=True)
        hidden_grad = prob * raw
        gg_ref[:, columns] = (hidden_grad * fac_ref[:, columns]).astype(bf16)
        ug_ref[:, columns] = (hidden_grad * act_ref[:, columns]).astype(bf16)
    logit_grad = prob_grad * prob * (1.0 - prob)
    lane = lax.broadcasted_iota(jnp.int32, stats_ref.shape, 1)
    lg_ref[...] = jnp.where(lane == 4, logit_grad, stats_ref[...])
    router_row = own_row(me_ref[0], router_ref)
    for start in range(0, width, step):
        part = slice(start, start + step)
        total = dot(gg_ref[...], gate_ref[part, :], ((1,), (1,)))
        total += dot(ug_ref[...], up_ref[part, :], ((1,), (1,)))
        put(backs, 0, (total + logit_grad * router_row[:, part]).astype(bf16), part)


def forward_kernel(number, me_ref, *refs):
    forward_body(me_ref, refs[:number], *refs[number:])


def forward(me, blocks, table, router, gate, up):
    count = sum(block.shape[0] for block in blocks)
    width, full = gate.shape
    wide = jax.ShapeDtypeStruct((count, full), f32)
    return pl.pallas_call(
        functools.partial(forward_kernel, len(blocks)),
        out_shape=[
            jax.ShapeDtypeStruct((count, width), bf16),
            jax.ShapeDtypeStruct((count, LANES), f32),
            wide,
            wide,
            jax.ShapeDtypeStruct((count, full), bf16),
        ],
        in_specs=[SMEM] + [VMEM] * (len(blocks) + 4),
        out_specs=[VMEM] * 5,
        compiler_params=params(12),
        cost_estimate=cost(4 * count * width * full, 4 * width * full + count * 12000),
        name="expert_in",
    )(me, *blocks, table, router, gate, up)


def backward_shapes(blocks, width, full):
    count = sum(block.shape[0] for block in blocks)
    return [jax.ShapeDtypeStruct((block.shape[0], width), bf16) for block in blocks] + [
        jax.ShapeDtypeStruct((count, 2 * width + 3 * full), bf16),
        jax.ShapeDtypeStruct((count, LANES), f32),
    ]


def backward_kernel(number, me_ref, *refs):
    cots, refs = refs[:number], refs[number:]
    table_ref, router_ref, seen_ref, stats_ref, act_ref, fac_ref, hid_ref, down_ref, gate_ref, up_ref = refs[:10]
    backs, (late_ref, lg_ref, ups_ref) = refs[10 : 10 + number], refs[10 + number :]
    mod, og, gg, ug, hid = late_views(late_ref, *gate_ref.shape)
    backward_body(0, me_ref, cots, table_ref, router_ref, stats_ref, act_ref, fac_ref, hid_ref, down_ref, gate_ref, up_ref, backs, og, gg, ug, lg_ref, ups_ref)
    mod[...] = seen_ref[...]
    hid[...] = hid_ref[...]


def backward(me, blocks, table, router, mod, stats, act, fac, hid, down, gate, up):
    count = sum(block.shape[0] for block in blocks)
    width, full = gate.shape
    number = len(blocks)
    outs = pl.pallas_call(
        functools.partial(backward_kernel, number),
        out_shape=backward_shapes(blocks, width, full),
        in_specs=[SMEM] + [VMEM] * (number + 10),
        out_specs=[VMEM] * (number + 2),
        scratch_shapes=[pltpu.VMEM((count, width), bf16)],
        compiler_params=params(12),
        cost_estimate=cost(6 * count * width * full, 6 * width * full + count * 16000),
        name="expert_back",
    )(me, *blocks, table, router, mod, stats, act, fac, hid, down, gate, up)
    return outs[:number], *outs[number:]


def whole_kernel(number, me_ref, *refs):
    blocks, refs = refs[:number], refs[number:]
    table_ref, router_ref, down_ref, gate_ref, up_ref = refs[:5]
    backs, refs = refs[5 : 5 + number], refs[5 + number :]
    late_ref, lg_ref, stats_ref, act_ref, fac_ref, ups_ref = refs
    mod, og, gg, ug, hid = late_views(late_ref, *gate_ref.shape)
    forward_body(me_ref, blocks, table_ref, router_ref, gate_ref, up_ref, mod, stats_ref, act_ref, fac_ref, hid)
    backward_body(mod.shape[1] + LANES, me_ref, blocks, table_ref, router_ref, stats_ref, act_ref, fac_ref, hid, down_ref, gate_ref, up_ref, backs, og, gg, ug, lg_ref, ups_ref)


def whole(me, blocks, table, router, down, gate, up):
    count = sum(block.shape[0] for block in blocks)
    width, full = gate.shape
    number = len(blocks)
    outs = pl.pallas_call(
        functools.partial(whole_kernel, number),
        out_shape=backward_shapes(blocks, width, full),
        in_specs=[SMEM] + [VMEM] * (number + 5),
        out_specs=[VMEM] * (number + 2),
        scratch_shapes=[pltpu.VMEM((count, LANES), f32)]
        + [pltpu.VMEM((count, full), f32)] * 2
        + [pltpu.VMEM((count, width), bf16)],
        compiler_params=params(16),
        cost_estimate=cost(10 * count * width * full, 6 * width * full + count * 16000),
        name="expert_whole",
    )(me, *blocks, table, router, down, gate, up)
    return outs[:number], *outs[number:]


def sums_kernel(numbers, tall, me_ref, *refs):
    rows, backs = [], []
    for group in (rows, backs):
        for number in numbers:
            group.append(refs[:number])
            refs = refs[number:]
    lates, stats = refs[:2], refs[2:4]
    meta_ref, cot_ref, mix_ref, out_ref = refs[4:]
    count, width = lates[0].shape[0], cot_ref.shape[1]
    conditions, experts = tall
    zero = ((0,), (0,))
    shift_sum = jnp.zeros((conditions, width), f32)
    scale_sum = jnp.zeros((conditions, width), f32)
    router_sum = jnp.zeros((1, width), f32)
    chunk = 128
    for q in range(2):
        for start in range(0, count, chunk):
            part = slice(start, start + chunk)
            lane = lax.broadcasted_iota(jnp.int32, (chunk, conditions), 1)
            mark = stats[q][part, 3:4].astype(jnp.int32)
            pick = (lane + 1 == mark).astype(f32).astype(bf16)
            back = piece(backs[q], start, chunk, slice(0, width))
            mean, inverse = stats[q][part, 0:1], stats[q][part, 1:2]
            values = piece(rows[q], start, chunk, slice(0, width)).astype(f32)
            normed = (values - mean) * inverse
            product = back.astype(f32) * normed
            high = product.astype(bf16)
            low = (product - high.astype(f32)).astype(bf16)
            shift_sum += dot(pick, back, zero)
            scale_sum += dot(pick, high, zero) + dot(pick, low, zero)
            weighted = stats[q][part, 4:5] * lates[q][part, :width].astype(f32)
            router_sum += jnp.sum(weighted, axis=0, keepdims=True)
    toks = cot_ref.shape[0]
    wanted = lax.broadcasted_iota(jnp.int32, (conditions, toks), 0)
    pick = (meta_ref[2:3, :] == wanted).astype(f32).astype(bf16)
    product = cot_ref[...].astype(f32) * mix_ref[...].astype(f32)
    high = product.astype(bf16)
    low = (product - high.astype(f32)).astype(bf16)
    out_ref[0:conditions, :] = shift_sum
    out_ref[conditions : 2 * conditions, :] = scale_sum
    out_ref[2 * conditions : 3 * conditions, :] = dot(pick, high) + dot(pick, low)
    place = lax.broadcasted_iota(jnp.int32, (out_ref.shape[0] - 3 * conditions, width), 0)
    out_ref[3 * conditions :, :] = jnp.where(place == me_ref[0], router_sum, 0.0)


def sums(me, rows, backs, lates, stats, meta, cot, mix, conditions, experts):
    numbers = [len(blocks) for blocks in rows]
    height = -(-(3 * conditions + experts) // 128) * 128
    width = cot.shape[1]
    return pl.pallas_call(
        functools.partial(sums_kernel, numbers, (conditions, experts)),
        out_shape=jax.ShapeDtypeStruct((height, width), f32),
        in_specs=[SMEM] + [VMEM] * (2 * sum(numbers) + 7),
        out_specs=VMEM,
        compiler_params=params(12),
        cost_estimate=cost(1e6, 1e4),
        name="table_sums",
    )(me, *rows[0], *rows[1], *backs[0], *backs[1], *lates, *stats, meta, cot, mix)


def grads_kernel(me_ref, near_ref, far_ref, *outs):
    width, half = outs[0].shape
    other_ref = outs[3]
    zero = ((0,), (0,))
    second = me_ref[2] != 0
    step = 256
    near, far = (late_views(ref, width, 2 * half) for ref in (near_ref, far_ref))
    for start in range(0, width, step):
        part = slice(start, start + step)
        for index, (left, right) in enumerate(((0, 2), (0, 3), (1, 4))):
            total = dot(near[left][:, part], near[right][...], zero)
            total += dot(far[left][:, part], far[right][...], zero)
            low, high = total[:, :half], total[:, half:]
            outs[index][part, :] = jnp.where(second, high, low).astype(bf16)
            other_ref[index, part, :] = jnp.where(second, low, high).astype(bf16)


def grads(me, lates, width, full):
    outs = pl.pallas_call(
        grads_kernel,
        out_shape=[jax.ShapeDtypeStruct((width, full // 2), bf16)] * 3
        + [jax.ShapeDtypeStruct((3, width, full // 2), bf16)],
        in_specs=[SMEM] + [VMEM] * 2,
        out_specs=[VMEM] * 4,
        compiler_params=params(12),
        cost_estimate=cost(1e6, 1e4),
        name="weight_grads",
    )(me, *lates)
    return outs[:3], outs[3]


def merge_kernel(count, cap, me_ref, meta_ref, *refs):
    picks = routing(me_ref[1], me_ref[0] - me_ref[1], meta_ref, count, cap).astype(bf16)
    rows = piece(refs[:-1], 0, count * cap, slice(None))
    refs[-1][...] = dot(picks, rows, ((0,), (0,))).astype(bf16)


def merge(me, meta, backs, cap):
    return pl.pallas_call(
        functools.partial(merge_kernel, len(backs), cap),
        out_shape=jax.ShapeDtypeStruct((meta.shape[1], backs[0].shape[1]), bf16),
        in_specs=[SMEM] + [VMEM] * (1 + len(backs)),
        out_specs=VMEM,
        compiler_params=params(8),
        cost_estimate=cost(1e9, 2e6),
        name="merge",
    )(me, meta, *backs)


def final_kernel(count, cap, me_ref, meta_ref, stamp_ref, tok_ref, cot_ref, table_ref, near_ref, far_ref, out_ref):
    picks = routing(me_ref[1], 0, meta_ref, count, cap).astype(bf16)
    mod_grad = dot(picks, near_ref[...], ((0,), (0,))) + far_ref[...].astype(f32)
    conditions = table_ref.shape[1]
    _, inverse, normed = normalize(tok_ref[...].astype(f32))
    pick = pick3((stamp_ref[:, 0:1] + 1).astype(f32), conditions)
    d_normed = mod_grad * (1.0 + dot(pick, split3(table_ref[1])))
    d_input = inverse * (
        d_normed
        - jnp.mean(d_normed, axis=-1, keepdims=True)
        - normed * jnp.mean(d_normed * normed, axis=-1, keepdims=True)
    )
    out_ref[...] = (cot_ref[...].astype(f32) + d_input).astype(bf16)


def final(me, meta, stamp_column, tokens, cot, table, near, far, count, cap):
    return pl.pallas_call(
        functools.partial(final_kernel, count, cap),
        out_shape=jax.ShapeDtypeStruct(tokens.shape, bf16),
        in_specs=[SMEM] + [VMEM] * 7,
        out_specs=VMEM,
        compiler_params=params(12),
        cost_estimate=cost(1e9, 4e6),
        name="final",
    )(me, meta, stamp_column, tokens, cot, table, near, far)


def rounded(values):
    return lax.reduce_precision(values, 8, 7)


def flip(values, name, size, bit):
    return lax.ppermute(values.astype(bf16), name, [(i, i ^ bit) for i in range(size)])


def scattered_axes(dp_axis, experts):
    return ([("dp", dp_axis, 1)] if dp_axis > 1 else []) + [("expert", experts, 1)]


def scatter_table(table, dp_axis, experts):
    for name, size, bit in scattered_axes(dp_axis, experts):
        high = (lax.axis_index(name) & bit) != 0
        rows = table.shape[0] // 2
        low_half, high_half = table[:rows], table[rows:]
        away = jnp.where(high, low_half, high_half)
        table = jnp.where(high, high_half, low_half)
        table = table + flip(away, name, size, bit).astype(f32)
    return table


def exchange_table(table, experts, first, last):
    bit = first
    while bit < last:
        table = rounded(table)
        table = table + flip(table, "expert", experts, bit).astype(f32)
        bit *= 2
    return table


def add_kernel(other_ref, *refs):
    number = len(refs) // 2
    for i in range(number):
        total = refs[i][...].astype(f32) + other_ref[i].astype(f32)
        refs[number + i][0] = total.astype(bf16)


def add(mine, other):
    width, half = mine[0].shape
    step = 256
    part = pl.BlockSpec((step, half), lambda i: (i, 0))
    return pl.pallas_call(
        add_kernel,
        grid=(width // step,),
        out_shape=[jax.ShapeDtypeStruct((1, width, half), bf16)] * len(mine),
        in_specs=[pl.BlockSpec((len(mine), step, half), lambda i: (0, i, 0))] + [part] * len(mine),
        out_specs=[pl.BlockSpec((1, step, half), lambda i: (0, i, 0))] * len(mine),
        compiler_params=params(12),
        cost_estimate=cost(1e6, 1e4),
        name="add",
    )(other, *mine)


def gather_table(table, dp_axis, experts):
    for name, size, bit in reversed(scattered_axes(dp_axis, experts)):
        high = (lax.axis_index(name) & bit) != 0
        other = flip(table, name, size, bit)
        table = jnp.concatenate(
            [jnp.where(high, other, table), jnp.where(high, table, other)], axis=0
        )
    return table


def local(experts, dp_axis, tokens, cotangent, mixture, stamp, expert_ids, modulation, router, w_gate, w_up, w_down):
    toks, width = tokens.shape
    conditions = modulation.shape[1]
    cap = min(toks, 4 * toks // experts)
    half = experts // 2
    index = lax.axis_index("expert").astype(jnp.int32)
    me = jnp.stack([index, index // half * half, lax.axis_index("dp").astype(jnp.int32)])
    halves = [list(range(half)), list(range(half, experts))]
    across = [(e, (e + half) % experts) for e in range(experts)]

    def hop(array):
        return lax.ppermute(array, "expert", across)

    def trade(array):
        blocks = array.reshape(half, cap, array.shape[1])
        blocks = lax.all_to_all(
            blocks, "expert", split_axis=0, concat_axis=0, tiled=True, axis_index_groups=halves
        )
        return blocks.reshape(array.shape)

    def fan(blocks):
        return [blocks[0]] + [
            lax.ppermute(blocks[k], "expert", [(e, e ^ k) for e in range(experts)])
            for k in range(1, half)
        ]

    def after(array, *others):
        return lax.optimization_barrier((array,) + others)[0]

    meta = jnp.concatenate(
        [expert_ids.T, stamp[None], jnp.zeros((5, toks), jnp.int32)], axis=0
    )
    gate, up, down = (
        lax.all_gather(w[0], "dp", axis=1, tiled=True) for w in (w_gate, w_up, w_down)
    )
    far_tokens = hop(tokens)
    far_meta = hop(meta)
    (near,) = pack(me, meta, [tokens, cotangent], True, False, half, cap)
    near, far_meta = lax.optimization_barrier((near, far_meta))
    near = trade(near)
    far_cot = hop(cotangent)
    far = pack(me, far_meta, [far_tokens], True, True, half, cap)
    far_cots = pack(me, far_meta, [far_cot], False, True, half, cap)
    far = fan(far)
    near, kept = lax.optimization_barrier((near, far_cots[0]))
    far_cots = [kept] + list(far_cots[1:])
    far_cots = fan(far_cots)

    near_backs, near_late, near_stats = whole(me, [near], modulation, router, down, gate, up)
    near_late, far = lax.optimization_barrier((near_late, far))
    far_in = forward(me, far, modulation, router, gate, up)
    far_backs, far_late, far_stats = backward(
        me, far_cots, modulation, router, *far_in, down, gate, up
    )
    far_back = fan(far_backs)
    lates = [near_late, far_late]
    table = sums(
        me, [[near], far], [near_backs, far_backs], lates, [near_stats, far_stats],
        meta, cotangent, mixture, conditions, experts,
    )
    mine, other = grads(me, lates, *gate.shape)
    merged = merge(me, far_meta, far_back, cap)
    merged, table, other = lax.optimization_barrier((merged, table, other))
    near_back = near_backs[0]
    far_grad = hop(merged)
    near_back = trade(near_back)
    other = lax.ppermute(other, "dp", [(i, dp_axis - 1 - i) for i in range(dp_axis)])
    table = scatter_table(table, dp_axis, experts)
    table = exchange_table(table, experts, 2, 2)
    d_gate, d_up, d_down = add(mine, other)
    table, near_back, far_grad, d_gate, d_up, d_down = lax.optimization_barrier(
        (table, near_back, far_grad, d_gate, d_up, d_down)
    )
    table = rounded(exchange_table(table, experts, 2, experts)).astype(bf16)
    table = gather_table(table, dp_axis, experts)
    d_tokens = final(
        me, meta, stamp[:, None], tokens, cotangent, modulation, near_back, far_grad, half, cap
    )
    table, d_tokens = lax.optimization_barrier((table, d_tokens))
    table = table.astype(f32)
    d_modulation = table[: 3 * conditions].reshape(3, conditions, width)
    d_router = table[3 * conditions : 3 * conditions + experts]
    return (d_tokens, d_gate, d_up, d_down, d_router, d_modulation)


def solution(mesh):
    return jax.shard_map(
        functools.partial(local, mesh.shape["expert"], mesh.shape["dp"]),
        mesh=mesh,
        in_specs=(
            P(("groups", "expert", "dp"), None),
            P(("groups", "expert", "dp"), None),
            P(("groups", "expert", "dp"), None),
            P(("groups", "expert", "dp")),
            P(("groups", "expert", "dp"), None),
            P(),
            P(),
            P("expert", None, "dp"),
            P("expert", None, "dp"),
            P("expert", None, "dp"),
        ),
        out_specs=(
            P(("groups", "expert", "dp"), None),
            P(("groups", "expert"), None, "dp"),
            P(("groups", "expert"), None, "dp"),
            P(("groups", "expert"), None, "dp"),
            P("groups", None),
            P(None, "groups", None),
        ),
        check_vma=False,
    )
```
